256 devices in a mesh: ctx: 32 (over z, x), tp: 8 (over y, core).
Axes of the slice: x: 4, y: 4, z: 8, core: 2. Of those that a mesh axis runs over, the one named last changes fastest.
Arguments:
- hyena_in: bfloat16 [6144, 3, 8192], P('ctx', None, 'tp'), may hold values from -6 to 6
- stream_in: bfloat16 [6144, 8192], P('ctx', 'tp'), may hold values from -12 to 12
- feat_filter: float32 [3, 3, 8192], P(None, None, 'tp'), may hold values from -3 to 3
- inner_filter: float32 [7, 8192], P(None, 'tp'), may hold values from -2.5 to 2.5
- queries: bfloat16 [6144, 8192], P('ctx', 'tp'), may hold values from -10 to 10
- key_vectors: bfloat16 [6144, 8192], P('ctx', 'tp'), may hold values from -4.1 to 4.1
- segments: int32 [6144], replicated, may hold values from 0 to 63, as said below
Outputs:
- stream: bfloat16 [6144, 8192], P('ctx', 'tp')
- attended: bfloat16 [6144, 8192], P('ctx', 'tp')
The draws below stay inside these ranges and needn't reach their ends.
Inputs may be any that keep to these rules, and one draw needn't show every extreme that they name: segments never fall; every document has 1 to 3072 tokens, and one has exactly 3072.
All inputs are finite; a program needn't handle non-finite values.
Results may differ from the reference program's by a relative error of at most 0.006.
Values may be sent and summed in bfloat16 or wider, within the bound.
A program may use at most 128 MiB of HBM per device.

```python
import math
import jax
import jax.numpy as jnp
from jax import lax

D = 8192
HEAD_DIM = 128
HEADS = 64
TOKENS = 6144
MOST = 3072
DOCS = 64


def document_segments(key):
    key = jax.random.fold_in(key, 13)
    weight_key, place_key = jax.random.split(key)
    count = DOCS - 1
    spare = TOKENS - MOST - count
    powers = jax.random.randint(weight_key, (count,), 0, 6, jnp.int32)
    weights = jnp.left_shift(jnp.ones((count,), jnp.int32), powers)
    extra = spare * weights // jnp.sum(weights)
    leftover = spare - jnp.sum(extra)
    extra = extra + (jnp.arange(count, dtype=jnp.int32) < leftover).astype(jnp.int32)
    others = (1 + extra).astype(jnp.int32)
    long_place = jax.random.randint(place_key, (), 0, DOCS, jnp.int32)
    index = jnp.arange(DOCS, dtype=jnp.int32)
    source = jnp.clip(index - (index > long_place).astype(jnp.int32), 0, count - 1)
    lengths = jnp.where(index == long_place, MOST, others[source]).astype(jnp.int32)
    ends = jnp.cumsum(lengths).astype(jnp.int32)
    positions = jnp.arange(TOKENS, dtype=jnp.int32)
    return jnp.sum((ends[None, :] <= positions[:, None]).astype(jnp.int32), axis=1).astype(jnp.int32)


def draw_segments(key, part):
    return document_segments(key)


def draw_stream_in(key, part):
    key = jax.random.fold_in(key, 3)
    base_key, row_key, col_key = jax.random.split(key, 3)
    columns = jnp.arange(D, dtype=jnp.float32) / D
    row_scale = 10.0 ** jax.random.uniform(row_key, (TOKENS, 1), jnp.float32, -0.5, 0.5)
    col_random = 10.0 ** jax.random.uniform(col_key, (1, D), jnp.float32, -0.25, 0.25)
    base = jnp.clip(jax.random.normal(base_key, (TOKENS, D), jnp.float32), -3.0, 3.0)
    rise = 3.0 ** (0.5 * (columns - 0.5))
    return (0.5 * base * row_scale * col_random * rise[None, :]).astype(jnp.bfloat16)


def draw_queries(key, part):
    base_key = jax.random.fold_in(jax.random.fold_in(key, 5), 0)
    result = jnp.clip(jax.random.normal(base_key, (TOKENS, D), jnp.float32), -4.0, 4.0)
    return result.astype(jnp.bfloat16)


def draw_key_vectors(key, part):
    base_key = jax.random.fold_in(key, 7)
    result = jnp.clip(jax.random.normal(base_key, (TOKENS, D), jnp.float32), -4.0, 4.0)
    return result.astype(jnp.bfloat16)


def levels(rng, extent, pieces, smallest, largest):
    level = 1.0
    for axis_at, shards_of in pieces:
        draws = jax.random.uniform(jax.random.fold_in(jax.random.fold_in(rng, 6), axis_at), (shards_of,), jnp.float32, smallest / len(pieces), largest / len(pieces))
        level = level * jnp.repeat(jnp.exp(draws), extent[axis_at] // shards_of).reshape((-1,) + (1,) * (len(extent) - 1 - axis_at))
    return level


def noise(rng, dims, spread, most, cuts=(), kind=jnp.bfloat16):
    values = jax.random.normal(rng, dims, jnp.float32) * spread
    if len(cuts) > 0:
        values = levels(rng, dims, cuts, -0.22, 0.18) * values
    return jnp.clip(values, min=-most, max=most).astype(kind)


def setup_inputs(seed: int = 0) -> dict:
    splits = jax.random.split(jax.random.key(seed), 8)
    return {
        "hyena_in": noise(splits[0], (TOKENS, 3, D), 1.0, 6.0, ((0, 32), (2, 8))),
        "stream_in": draw_stream_in(jax.random.fold_in(splits[7], 71), 0),
        "feat_filter": noise(splits[2], (3, 3, D), 0.6, 3.0, ((2, 8),), jnp.float32),
        "inner_filter": noise(splits[3], (7, D), 0.4, 2.5, ((1, 8),), jnp.float32),
        "queries": draw_queries(jax.random.fold_in(splits[7], 71), 0),
        "key_vectors": draw_key_vectors(jax.random.fold_in(splits[7], 71), 0),
        "segments": draw_segments(jax.random.fold_in(splits[7], 71), 0),
    }


def apply_taps(series, segs, taps, out_rows):
    total_rows = series.shape[0]
    offset = total_rows - out_rows
    seg_here = segs[offset:]
    result = jnp.zeros((out_rows,) + series.shape[1:], series.dtype)
    for tap_index in range(taps.shape[0]):
        lower_row = offset - tap_index
        shifted = series[lower_row:lower_row + out_rows]
        same_doc = (segs[lower_row:lower_row + out_rows] == seg_here).astype(series.dtype)
        same_doc = same_doc.reshape((out_rows,) + (1,) * (series.ndim - 1))
        result = result + taps[tap_index] * shifted * same_doc
    return result

def causal_conv(series, segments, taps):
    rim_depth = taps.shape[0] - 1
    padded = jnp.concatenate([jnp.zeros((rim_depth,) + series.shape[1:], series.dtype), series])
    segs = jnp.concatenate([jnp.full((rim_depth,), -1, jnp.int32), segments.astype(jnp.int32)])
    return apply_taps(padded, segs, taps, series.shape[0])

def attend_head(q_head, k_head, v_head, segments):
    block_rows = math.gcd(512, TOKENS)
    key_span = min(TOKENS, TOKENS // 2 + block_rows)
    inv_root = 1.0 / math.sqrt(HEAD_DIM)

    def one_block(block_index):
        q_start = block_index * block_rows
        k_start = jnp.clip(q_start + block_rows - key_span, 0, TOKENS - key_span).astype(jnp.int32)
        q_block = lax.dynamic_slice_in_dim(q_head, q_start, block_rows)
        k_block = lax.dynamic_slice_in_dim(k_head, k_start, key_span)
        v_block = lax.dynamic_slice_in_dim(v_head, k_start, key_span)
        seg_query = lax.dynamic_slice_in_dim(segments, q_start, block_rows)
        seg_key = lax.dynamic_slice_in_dim(segments, k_start, key_span)
        query_pos = q_start + jnp.arange(block_rows, dtype=jnp.int32)
        key_pos = k_start + jnp.arange(key_span, dtype=jnp.int32)
        scores = jnp.dot(q_block, k_block.T, preferred_element_type=jnp.float32) * inv_root
        allowed = (seg_query[:, None] == seg_key[None, :]) & (key_pos[None, :] <= query_pos[:, None])
        row_top = lax.optimization_barrier(jnp.max(jnp.where(allowed, scores, -1e+30), axis=1))
        exp_terms = jnp.where(allowed, jnp.exp(scores - row_top[:, None]), 0.0)
        totals = lax.optimization_barrier(jnp.sum(exp_terms, axis=1))
        summed = jnp.dot(exp_terms.astype(jnp.bfloat16), v_block, preferred_element_type=jnp.float32)
        return (summed / totals[:, None]).astype(jnp.bfloat16)
    blocks = lax.map(one_block, jnp.arange(TOKENS // block_rows, dtype=jnp.int32))
    return blocks.reshape(TOKENS, HEAD_DIM)

def reference(hyena_in, stream_in, feat_filter, inner_filter, queries, key_vectors, segments):
    featured = causal_conv(hyena_in.astype(jnp.float32), segments, feat_filter)
    product = featured[:, 1] * featured[:, 2]
    mixing = causal_conv(product, segments, inner_filter)
    stream = (stream_in.astype(jnp.float32) + featured[:, 0] * mixing).astype(jnp.bfloat16)
    widened = stream.astype(jnp.float32)
    norm_scale = lax.rsqrt(lax.optimization_barrier(jnp.mean(widened * widened, axis=1)) + 1e-05)
    values = (widened * norm_scale[:, None]).astype(jnp.bfloat16)

    def by_head(arr):
        return arr.reshape(TOKENS, HEADS, HEAD_DIM).transpose(1, 0, 2)
    per_head = lax.map(lambda triple: attend_head(triple[0], triple[1], triple[2], segments), (by_head(queries), by_head(key_vectors), by_head(values)))
    attended = per_head.transpose(1, 0, 2).reshape(TOKENS, D)
    return (stream, attended)
```

```python
import functools
import math

import jax
import jax.numpy as jnp
from jax import lax
from jax.experimental import pallas as pl
from jax.experimental.pallas import tpu as pltpu
from jax.sharding import PartitionSpec as P

HEAD_DIM = 128
HALO = 16
EPSILON = 1e-05
BIG = 1e30
MESH = pl.DeviceIdType.MESH
F32 = jnp.float32
BF16 = jnp.bfloat16
RING_X = 4


def ring_offsets(count):
    offsets = [0]
    for distance in range(1, count // 2 + 1):
        offsets.append(distance)
        if distance != count - distance:
            offsets.append(-distance)
    return offsets


def slot_of(delta, count):
    ahead = jnp.maximum(2 * delta - 1, 0)
    return jnp.where(delta <= count // 2, ahead, 2 * (count - delta))


def front_kernel(
    ring_z, ring_tp, rows,
    hyena, stream_in, feat, inner, queries, keys, seg,
    stream_out, q_all, k_all, v_all,
    hyena_buf, wide, product, gate_free, stream_buf, values, segcol, sums, total_col, in_buf,
    load_sem, own_sem, halo_sem, sum_send, sum_recv,
    z_send, z_recv, x_send, x_recv, far_send, far_recv,
):
    ctx = lax.axis_index("ctx")
    tp = lax.axis_index("tp")
    z = ctx // RING_X
    x = ctx % RING_X
    ring_ctx = ring_z * RING_X
    channels = queries.shape[1]
    offsets = ring_offsets(ring_z)
    half = rows // 2
    right = (x + 1) % RING_X
    left = (x + RING_X - 1) % RING_X
    far = (x + 2) % RING_X
    right_id = (z * RING_X + right, tp)
    left_id = (z * RING_X + left, tp)
    next_ctx = (ctx + 1) % ring_ctx
    prev_ctx = (ctx + ring_ctx - 1) % ring_ctx

    def z_at(offset):
        return (z + offset + ring_z) % ring_z

    def head_cols(index):
        return pl.ds(pl.multiple_of(index * HEAD_DIM, HEAD_DIM), HEAD_DIM)

    load_h = pltpu.make_async_copy(hyena, hyena_buf.at[:, pl.ds(HALO, rows)], load_sem.at[0])
    load_s = pltpu.make_async_copy(stream_in, in_buf, load_sem.at[1])
    load_h.start()
    load_s.start()
    own_k = pltpu.make_async_copy(keys.at[:, head_cols(z)], k_all.at[0, x], own_sem.at[0])
    own_q = pltpu.make_async_copy(queries.at[:, head_cols(z)], q_all.at[0], own_sem.at[1])
    own_k.start()
    own_q.start()

    barrier = pltpu.get_barrier_semaphore()
    partners = [(z_at(offset) * RING_X + x, tp) for offset in offsets[1:]]
    partners += [right_id, left_id, (next_ctx, tp), (prev_ctx, tp)]
    partners += [(ctx, (tp + step) % ring_tp) for step in range(1, ring_tp)]
    for partner in partners:
        pl.semaphore_signal(barrier, inc=1, device_id=partner, device_id_type=MESH)

    def seg_row(row, carry):
        token = ctx * rows - HALO + row
        number = jnp.where(token >= 0, seg[jnp.maximum(token, 0)], -1)
        segcol[pl.ds(row, 1), :] = jnp.full((1, 128), number, jnp.int32)
        return carry

    lax.fori_loop(0, HALO + rows, seg_row, 0)

    pl.semaphore_wait(barrier, len(partners))

    halo = pltpu.make_async_remote_copy(
        src_ref=hyena.at[:, pl.ds(rows - HALO, HALO)],
        dst_ref=hyena_buf.at[:, pl.ds(0, HALO)],
        send_sem=halo_sem.at[0], recv_sem=halo_sem.at[1],
        device_id=(next_ctx, tp), device_id_type=MESH,
    )
    halo.start()

    def z_copy(kind, slot, source, target):
        goal = z_at(-offsets[slot])
        return pltpu.make_async_remote_copy(
            src_ref=source.at[:, head_cols(goal)], dst_ref=target,
            send_sem=z_send.at[kind, slot], recv_sem=z_recv.at[kind, slot],
            device_id=(goal * RING_X + x, tp), device_id_type=MESH,
        )

    k_copies = [z_copy(0, slot, keys, k_all.at[slot, x]) for slot in range(1, ring_z)]
    for copy in k_copies:
        copy.start()

    load_h.wait()
    load_s.wait()
    wide[:, pl.ds(HALO, rows)] = hyena_buf[:, pl.ds(HALO, rows)].astype(F32)
    halo.wait_recv()
    wide[:, pl.ds(0, HALO)] = hyena_buf[:, pl.ds(0, HALO)].astype(F32)
    feat_taps, inner_taps = feat.shape[0], inner.shape[0]

    def tile_lanes(mask):
        return jnp.concatenate([mask] * (channels // 128), axis=1)

    def featured(group, start, count, masks):
        result = None
        for tap in range(feat_taps):
            term = feat[tap, group][None, :] * wide[group, pl.ds(start - tap, count), :]
            if tap > 0:
                term = term * masks[tap]
            result = term if result is None else result + term
        return result

    def masks_of(start, count, taps):
        here = segcol[pl.ds(start, count), :]
        return [None] + [
            tile_lanes((segcol[pl.ds(start - tap, count), :] == here).astype(F32))
            for tap in range(1, taps)
        ]

    masks = masks_of(8, 8, feat_taps)
    product[pl.ds(8, 8), :] = featured(1, 8, 8, masks) * featured(2, 8, 8, masks)

    for start in range(HALO, HALO + rows, 8):
        masks = masks_of(start, 8, inner_taps)
        key_value = featured(1, start, 8, masks) * featured(2, start, 8, masks)
        product[pl.ds(start, 8), :] = key_value
        mixing = inner[0][None, :] * key_value
        for tap in range(1, inner_taps):
            mixing = mixing + inner[tap][None, :] * product[pl.ds(start - tap, 8), :] * masks[tap]
        gate_free[pl.ds(start - HALO, 8), :] = featured(0, start, 8, masks) * mixing

    for start in range(0, rows, 16):
        stream = (in_buf[pl.ds(start, 16), :].astype(F32) + gate_free[pl.ds(start, 16), :]).astype(BF16)
        stream_buf[pl.ds(start, 16), :] = stream
        stream = stream.astype(F32)
        square = stream * stream
        folded = square[:, 0:128]
        for lane in range(128, channels, 128):
            folded = folded + square[:, lane:lane + 128]
        total_col[pl.ds(start, 16), :] = folded
    store_s = pltpu.make_async_copy(stream_buf, stream_out, load_sem.at[0])
    store_s.start()

    padded = total_col.shape[0]
    if padded > rows:
        total_col[pl.ds(rows, padded - rows), :] = jnp.zeros((padded - rows, 128), F32)
    for start in range(0, padded, 128):
        turned = total_col[pl.ds(start, 128), :].T
        row = jnp.sum(turned, axis=0, keepdims=True)
        sums[tp, :, pl.ds(start, 128)] = jnp.broadcast_to(row, (8, 128))
    sum_copies = []
    for step in range(1, ring_tp):
        copy = pltpu.make_async_remote_copy(
            src_ref=sums.at[tp], dst_ref=sums.at[tp],
            send_sem=sum_send.at[step], recv_sem=sum_recv.at[step],
            device_id=(ctx, (tp + step) % ring_tp), device_id_type=MESH,
        )
        copy.start()
        sum_copies.append(copy)

    groups = [(0, 1)] + [(lo, min(lo + 2, ring_z)) for lo in range(1, ring_z, 2)]

    def near_copy(kind, group, way, array):
        lo, hi = groups[group]
        return pltpu.make_async_remote_copy(
            src_ref=array.at[pl.ds(lo, hi - lo), x], dst_ref=array.at[pl.ds(lo, hi - lo), x],
            send_sem=x_send.at[kind, group, way], recv_sem=x_recv.at[kind, group, way],
            device_id=(right_id, left_id)[way], device_id_type=MESH,
        )

    def near_wait(kind, group, way, array):
        lo, hi = groups[group]
        source = (left, right)[way]
        pltpu.make_async_remote_copy(
            src_ref=array.at[pl.ds(lo, hi - lo), source], dst_ref=array.at[pl.ds(lo, hi - lo), source],
            send_sem=x_send.at[kind, group, way], recv_sem=x_recv.at[kind, group, way],
            device_id=(right_id, left_id)[way], device_id_type=MESH,
        ).wait_recv()

    def far_copy(kind, group, way, array):
        lo, hi = groups[group]
        source = (left, right)[way]
        view = array.at[pl.ds(lo, hi - lo), source, pl.ds(way * half, half)]
        return pltpu.make_async_remote_copy(
            src_ref=view, dst_ref=view,
            send_sem=far_send.at[kind, group, way], recv_sem=far_recv.at[kind, group, way],
            device_id=(right_id, left_id)[way], device_id_type=MESH,
        )

    def far_wait(kind, group, way, array):
        lo, hi = groups[group]
        view = array.at[pl.ds(lo, hi - lo), far, pl.ds(way * half, half)]
        pltpu.make_async_remote_copy(
            src_ref=view, dst_ref=view,
            send_sem=far_send.at[kind, group, way], recv_sem=far_recv.at[kind, group, way],
            device_id=(right_id, left_id)[way], device_id_type=MESH,
        ).wait_recv()

    x_copies = []

    def first_hops(kind, array, z_copies, own):
        for group, (lo, hi) in enumerate(groups):
            if lo == 0:
                own.wait()
            else:
                for slot in range(lo, hi):
                    z_copies[slot - 1].wait_recv()
            for way in range(2):
                copy = near_copy(kind, group, way, array)
                copy.start()
                x_copies.append(copy)

    def second_hops(kind, array):
        for group in range(len(groups)):
            for way in range(2):
                near_wait(kind, group, way, array)
                copy = far_copy(kind, group, way, array)
                copy.start()
                x_copies.append(copy)

    first_hops(0, k_all, k_copies, own_k)

    total = sums[tp]
    for step in range(1, ring_tp):
        sum_copies[step - 1].wait_recv()
    for step in range(1, ring_tp):
        total = total + sums[(tp + step) % ring_tp]
    scale = lax.rsqrt(total / (channels * ring_tp) + EPSILON)
    for start in range(0, padded, 128):
        row = jnp.broadcast_to(scale[0:1, start:start + 128], (128, 128))
        total_col[pl.ds(start, 128), :] = row.T
    for start in range(0, rows, 16):
        norm = tile_lanes(total_col[pl.ds(start, 16), :])
        values[pl.ds(start, 16), :] = (stream_buf[pl.ds(start, 16), :].astype(F32) * norm).astype(BF16)

    v_copies = [z_copy(1, slot, values, v_all.at[slot, x]) for slot in range(1, ring_z)]
    for copy in v_copies:
        copy.start()
    own_v = pltpu.make_async_copy(values.at[:, head_cols(z)], v_all.at[0, x], own_sem.at[2])
    own_v.start()
    q_copies = [z_copy(2, slot, queries, q_all.at[slot]) for slot in range(1, ring_z)]
    for copy in q_copies:
        copy.start()

    second_hops(0, k_all)
    first_hops(1, v_all, v_copies, own_v)
    second_hops(1, v_all)
    own_q.wait()
    store_s.wait()
    for copy in q_copies:
        copy.wait_recv()
    for kind, array in ((0, k_all), (1, v_all)):
        for group in range(len(groups)):
            for way in range(2):
                far_wait(kind, group, way, array)
    halo.wait_send()
    for copy in sum_copies + k_copies + v_copies + q_copies + x_copies:
        copy.wait_send()


def attend_kernel(ring_z, tile_rows, seg, seg_lanes, q_all, k_all, v_all, out, scores_buf):
    ctx = lax.axis_index("ctx")
    z = ctx // RING_X
    x = ctx % RING_X
    rows = q_all.shape[1]
    tile = tile_rows
    per_z = RING_X * rows // tile
    blocks = tile // rows
    factor = math.log2(math.e) / math.sqrt(HEAD_DIM)
    last_token = seg.shape[0]
    steps = max(1, last_token.bit_length())
    lane_rows = tile // 128

    def key_tile(array, index):
        row_z = index // per_z
        slot = slot_of((row_z - z + ring_z) % ring_z, ring_z)
        part = index % per_z
        return array[slot, pl.ds(part * blocks, blocks)].reshape(tile, HEAD_DIM)

    def documents(index):
        return jnp.concatenate(
            [seg_lanes[pl.ds(index * lane_rows + i, 1), :] for i in range(lane_rows)], axis=1
        )

    numbers = lax.broadcasted_iota(jnp.int32, (128, tile), 0)

    for row_z in range(ring_z):
        block = row_z * RING_X + x
        first = block * rows
        slot = slot_of((row_z - z + ring_z) % ring_z, ring_z)
        first_doc = seg[first]
        last_doc = seg[first + rows - 1]

        def search(_, bounds):
            low, high = bounds
            mid = (low + high) // 2
            before = (seg[jnp.minimum(mid, last_token - 1)] < first_doc) & (low < high)
            return jnp.where(before, mid + 1, low), jnp.where(before | (low >= high), high, mid)

        low, _ = lax.fori_loop(0, steps, search, (0, first))
        lo_tile = low // tile
        hi_tile = first // tile
        q = q_all[slot]
        hits = (numbers == documents(hi_tile)).astype(F32)
        in_tile = first - hi_tile * tile

        q_docs = lax.cond(
            in_tile == 0,
            lambda: hits[:, 0:rows],
            lambda: hits[:, tile - rows:tile],
        )
        q_miss = (1.0 - q_docs).T.astype(BF16)

        def raw_scores(index):
            return lax.dot_general(
                q, key_tile(k_all, index), (((1,), (1,)), ((), ())), preferred_element_type=F32
            )

        def penalty(index):
            k_docs = jnp.where(numbers == documents(index), -BIG, 0.0).astype(BF16)
            return jnp.dot(q_miss, k_docs, preferred_element_type=F32)

        def fold_max(top, scores):
            for lane in range(0, tile, 128):
                top = jnp.maximum(top, scores[:, lane:lane + 128])
            return top

        def score_tile(index, top):
            scores = lax.cond(
                seg[index * tile] != last_doc,
                lambda: raw_scores(index) + penalty(index),
                lambda: raw_scores(index),
            )
            scores_buf[index - lo_tile] = scores
            return fold_max(top, scores)

        top = lax.fori_loop(lo_tile, hi_tile, score_tile, jnp.full((rows, 128), -BIG, F32))
        scores = raw_scores(hi_tile) + penalty(hi_tile)
        row_at = in_tile + lax.broadcasted_iota(jnp.int32, (rows, tile), 0)
        col_at = lax.broadcasted_iota(jnp.int32, (rows, tile), 1)
        scores = jnp.where(col_at <= row_at, scores, -BIG)
        scores_buf[hi_tile - lo_tile] = scores
        top = jnp.max(fold_max(top, scores), axis=1, keepdims=True)

        def weigh_tile(index, carry):
            sums, summed = carry
            terms = jnp.exp2((scores_buf[index - lo_tile] - top) * factor)
            for lane in range(0, tile, 128):
                sums = sums + terms[:, lane:lane + 128]
            summed = summed + jnp.dot(
                terms.astype(BF16), key_tile(v_all, index), preferred_element_type=F32
            )
            return sums, summed

        sums, summed = lax.fori_loop(
            lo_tile, hi_tile + 1, weigh_tile,
            (jnp.zeros((rows, 128), F32), jnp.zeros((rows, HEAD_DIM), F32)),
        )
        out[slot] = (summed / jnp.sum(sums, axis=1, keepdims=True)).astype(BF16)


def return_kernel(ring_z, results, attended, own_sem, send_sem, recv_sem):
    ctx = lax.axis_index("ctx")
    tp = lax.axis_index("tp")
    z = ctx // RING_X
    x = ctx % RING_X
    offsets = ring_offsets(ring_z)

    def z_at(offset):
        return (z + offset + ring_z) % ring_z

    def head_cols(index):
        return pl.ds(pl.multiple_of(index * HEAD_DIM, HEAD_DIM), HEAD_DIM)

    own = pltpu.make_async_copy(results.at[0], attended.at[:, head_cols(z)], own_sem)
    own.start()
    barrier = pltpu.get_barrier_semaphore()
    partners = [(z_at(offset) * RING_X + x, tp) for offset in offsets[1:]]
    for partner in partners:
        pl.semaphore_signal(barrier, inc=1, device_id=partner, device_id_type=MESH)
    pl.semaphore_wait(barrier, len(partners))
    copies = []
    for slot in range(1, ring_z):
        copy = pltpu.make_async_remote_copy(
            src_ref=results.at[slot], dst_ref=attended.at[:, head_cols(z)],
            send_sem=send_sem.at[slot], recv_sem=recv_sem.at[slot],
            device_id=(z_at(offsets[slot]) * RING_X + x, tp), device_id_type=MESH,
        )
        copy.start()
        copies.append(copy)
    own.wait()
    for slot in range(1, ring_z):
        view = attended.at[:, head_cols(z_at(-offsets[slot]))]
        pltpu.make_async_remote_copy(
            src_ref=results.at[slot], dst_ref=view,
            send_sem=send_sem.at[slot], recv_sem=recv_sem.at[slot],
            device_id=(z_at(offsets[slot]) * RING_X + x, tp), device_id_type=MESH,
        ).wait_recv()
    for copy in copies:
        copy.wait_send()


ANY = pl.BlockSpec(memory_space=pl.ANY)
VMEM = pl.BlockSpec(memory_space=pltpu.VMEM)
SMEM = pl.BlockSpec(memory_space=pltpu.SMEM)


def body(ring_ctx, ring_tp, most, hyena_in, stream_in, feat_filter, inner_filter, queries, key_vectors, segments):
    rows, channels = stream_in.shape
    ring_z = ring_ctx // RING_X
    tokens = segments.shape[0]
    hyena = jnp.transpose(hyena_in, (1, 0, 2))
    padded = -(-rows // 128) * 128
    dma = pltpu.SemaphoreType.DMA
    gathered = jax.ShapeDtypeStruct((ring_z, RING_X, rows, HEAD_DIM), BF16)
    group_count = 1 + ring_z // 2
    stream, q_all, k_all, v_all = pl.pallas_call(
        functools.partial(front_kernel, ring_z, ring_tp, rows),
        name="front",
        out_shape=(
            jax.ShapeDtypeStruct((rows, channels), BF16),
            jax.ShapeDtypeStruct((ring_z, rows, HEAD_DIM), BF16),
            gathered,
            gathered,
        ),
        in_specs=[ANY, ANY, VMEM, VMEM, ANY, ANY, SMEM],
        out_specs=(ANY, ANY, ANY, ANY),
        scratch_shapes=[
            pltpu.VMEM((3, HALO + rows, channels), BF16),
            pltpu.VMEM((3, HALO + rows, channels), F32),
            pltpu.VMEM((HALO + rows, channels), F32),
            pltpu.VMEM((rows, channels), F32),
            pltpu.VMEM((rows, channels), BF16),
            pltpu.VMEM((rows, channels), BF16),
            pltpu.VMEM((HALO + rows, 128), jnp.int32),
            pltpu.VMEM((ring_tp, 8, padded), F32),
            pltpu.VMEM((padded, 128), F32),
            pltpu.VMEM((rows, channels), BF16),
            dma((2,)), dma((3,)), dma((2,)), dma((ring_tp,)), dma((ring_tp,)),
            dma((3, ring_z)), dma((3, ring_z)),
            dma((2, group_count, 2)), dma((2, group_count, 2)),
            dma((2, group_count, 2)), dma((2, group_count, 2)),
        ],
        compiler_params=pltpu.CompilerParams(
            collective_id=0, has_side_effects=True, vmem_limit_bytes=32 * 1024 * 1024
        ),
    )(hyena, stream_in, feat_filter, inner_filter, queries, key_vectors, segments)

    tile = 2 * rows
    seg_lanes = segments.reshape(tokens // 128, 128)
    results = pl.pallas_call(
        functools.partial(attend_kernel, ring_z, tile),
        name="attend",
        out_shape=jax.ShapeDtypeStruct((ring_z, rows, HEAD_DIM), BF16),
        in_specs=[SMEM, VMEM, VMEM, VMEM, VMEM],
        out_specs=VMEM,
        scratch_shapes=[pltpu.VMEM((most // tile + 2, rows, tile), F32)],
        compiler_params=pltpu.CompilerParams(vmem_limit_bytes=32 * 1024 * 1024),
    )(segments, seg_lanes, q_all, k_all, v_all)

    attended = pl.pallas_call(
        functools.partial(return_kernel, ring_z),
        name="give_back",
        out_shape=jax.ShapeDtypeStruct((rows, channels), BF16),
        in_specs=[ANY],
        out_specs=ANY,
        scratch_shapes=[dma, dma((ring_z,)), dma((ring_z,))],
        compiler_params=pltpu.CompilerParams(collective_id=1, has_side_effects=True),
    )(results)
    return stream, attended


def solution(mesh):
    in_specs = (
        P("ctx", None, "tp"),
        P("ctx", "tp"),
        P(None, None, "tp"),
        P(None, "tp"),
        P("ctx", "tp"),
        P("ctx", "tp"),
        P(),
    )
    out_specs = (P("ctx", "tp"), P("ctx", "tp"))

    def whole(*args):
        most = args[-1].shape[0] // 2
        mapped = jax.shard_map(
            functools.partial(body, mesh.shape["ctx"], mesh.shape["tp"], most),
            mesh=mesh, in_specs=in_specs, out_specs=out_specs, check_vma=False,
        )
        return mapped(*args)

    return whole
```

```python
import functools
import math

import jax
import jax.numpy as jnp
from jax import lax
from jax.experimental import pallas as pl
from jax.experimental.pallas import tpu as pltpu
from jax.sharding import PartitionSpec as P

HEAD_DIM = 128
HALO = 16
EPSILON = 1e-05
BIG = 1e30
CHUNK = 64
MESH = pl.DeviceIdType.MESH
F32 = jnp.float32
BF16 = jnp.bfloat16
RING_X = 4


def ring_offsets(count):
    offsets = [0]
    for distance in range(1, count // 2 + 1):
        offsets.append(distance)
        if distance != count - distance:
            offsets.append(-distance)
    return offsets


def slot_of(delta, count):
    ahead = jnp.maximum(2 * delta - 1, 0)
    return jnp.where(delta <= count // 2, ahead, 2 * (count - delta))


def mixer_kernel(
    ring_z, ring_tp, rows, most,
    hyena, stream_in, feat_in, inner_in, queries, keys, seg,
    stream_out, attended,
    hyena_buf, wide, product, gate_free, in_buf, stream_buf, values, feat, inner,
    seg_buf, turn_buf, seg_col, seg_query, sums, total_col,
    q_all, k_all, v_all, scores_buf, terms_buf, inverse, summed, results,
    load_sem, own_sem, halo_sem, sum_send, sum_recv,
    z_send, z_recv, x_send, x_recv, far_send, far_recv, back_send, back_recv,
):
    ctx = lax.axis_index("ctx")
    tp = lax.axis_index("tp")
    z = ctx // RING_X
    x = ctx % RING_X
    ring_ctx = ring_z * RING_X
    channels = queries.shape[1]
    offsets = ring_offsets(ring_z)
    half = rows // 2
    right = (x + 1) % RING_X
    left = (x + RING_X - 1) % RING_X
    far = (x + 2) % RING_X
    right_id = (z * RING_X + right, tp)
    left_id = (z * RING_X + left, tp)
    next_ctx = (ctx + 1) % ring_ctx
    prev_ctx = (ctx + ring_ctx - 1) % ring_ctx
    span = RING_X * rows
    reach = -(-most // span)
    lane_rows = span // 128
    turns = turn_buf.shape[0] // 128
    factor = math.log2(math.e) / math.sqrt(HEAD_DIM)

    def z_at(offset):
        return (z + offset + ring_z) % ring_z

    def head_cols(index):
        return pl.ds(pl.multiple_of(index * HEAD_DIM, HEAD_DIM), HEAD_DIM)

    loads = [
        pltpu.make_async_copy(source, target, load_sem.at[index])
        for index, (source, target) in enumerate((
            (seg, seg_buf),
            (feat_in, feat),
            (inner_in, inner),
            (hyena, hyena_buf.at[:, pl.ds(HALO, rows)]),
            (stream_in, in_buf),
        ))
    ]
    own_k = pltpu.make_async_copy(keys.at[:, head_cols(z)], k_all.at[0, x], own_sem.at[0])
    own_q = pltpu.make_async_copy(queries.at[:, head_cols(z)], q_all.at[0], own_sem.at[1])

    barrier = pltpu.get_barrier_semaphore()
    partners = [(z_at(offset) * RING_X + x, tp) for offset in offsets[1:]]
    partners += [right_id, left_id, (next_ctx, tp), (prev_ctx, tp)]
    partners += [(ctx, (tp + step) % ring_tp) for step in range(1, ring_tp)]
    for partner in partners:
        pl.semaphore_signal(barrier, inc=1, device_id=partner, device_id_type=MESH)
    for load in loads:
        load.start()
    own_k.start()
    own_q.start()

    def columns(block):
        first = block * rows
        top_row = first // 128 - 1
        for turn in range(turns):
            row = seg_buf[pl.ds(jnp.maximum(top_row + turn, 0), 1), :].astype(F32)
            turn_buf[pl.ds(turn * 128, 128), :] = jnp.broadcast_to(row, (128, 128)).T
        return pl.multiple_of(first - top_row * 128, 16)

    loads[0].wait()
    start_at = columns(ctx)
    seg_col[...] = turn_buf[pl.ds(start_at - HALO, HALO + rows), :]
    seg_col[pl.ds(0, HALO), :] = jnp.where(ctx == 0, -1.0, seg_col[pl.ds(0, HALO), :])
    seg_query[0] = seg_col[pl.ds(HALO, rows), :]

    pl.semaphore_wait(barrier, len(partners))

    halo = pltpu.make_async_remote_copy(
        src_ref=hyena.at[:, pl.ds(rows - HALO, HALO)],
        dst_ref=hyena_buf.at[:, pl.ds(0, HALO)],
        send_sem=halo_sem.at[0], recv_sem=halo_sem.at[1],
        device_id=(next_ctx, tp), device_id_type=MESH,
    )
    halo.start()

    def z_copy(kind, slot, source, target):
        goal = z_at(-offsets[slot])
        return pltpu.make_async_remote_copy(
            src_ref=source.at[:, head_cols(goal)], dst_ref=target,
            send_sem=z_send.at[kind, slot], recv_sem=z_recv.at[kind, slot],
            device_id=(goal * RING_X + x, tp), device_id_type=MESH,
        )

    k_copies = [z_copy(0, slot, keys, k_all.at[slot, x]) for slot in range(1, ring_z)]
    for copy in k_copies:
        copy.start()
    v_copies = [z_copy(1, slot, values, v_all.at[slot, x]) for slot in range(1, ring_z)]
    own_v = pltpu.make_async_copy(values.at[:, head_cols(z)], v_all.at[0, x], own_sem.at[2])
    q_copies = [z_copy(2, slot, queries, q_all.at[slot]) for slot in range(1, ring_z)]

    groups = [(0, 1)] + [(lo, min(lo + 2, ring_z)) for lo in range(1, ring_z, 2)]
    last_group = len(groups) - 1
    x_copies = []

    def near(kind, group, way, array, source):
        lo, hi = groups[group]
        view = array.at[pl.ds(lo, hi - lo), source]
        return pltpu.make_async_remote_copy(
            src_ref=view, dst_ref=view,
            send_sem=x_send.at[kind, group, way], recv_sem=x_recv.at[kind, group, way],
            device_id=(right_id, left_id)[way], device_id_type=MESH,
        )

    def further(kind, group, way, array, source):
        lo, hi = groups[group]
        view = array.at[pl.ds(lo, hi - lo), source, pl.ds(way * half, half)]
        return pltpu.make_async_remote_copy(
            src_ref=view, dst_ref=view,
            send_sem=far_send.at[kind, group, way], recv_sem=far_recv.at[kind, group, way],
            device_id=(right_id, left_id)[way], device_id_type=MESH,
        )

    def first_hop(kind, group):
        array, copies, own = ((k_all, k_copies, own_k), (v_all, v_copies, own_v))[kind]
        lo, hi = groups[group]
        if lo == 0:
            own.wait()
        else:
            for slot in range(lo, hi):
                copies[slot - 1].wait_recv()
        for way in range(2):
            copy = near(kind, group, way, array, x)
            copy.start()
            x_copies.append(copy)

    def second_hop(kind, group):
        array = (k_all, v_all)[kind]
        for way in range(2):
            near(kind, group, way, array, (left, right)[way]).wait_recv()
            copy = further(kind, group, way, array, (left, right)[way])
            copy.start()
            x_copies.append(copy)

    def arrived(kind):
        for group in range(len(groups)):
            for way in range(2):
                further(kind, group, way, (k_all, v_all)[kind], far).wait_recv()

    first_hop(0, 0)

    for load in loads[1:]:
        load.wait()
    wide[:, pl.ds(HALO, rows)] = hyena_buf[:, pl.ds(HALO, rows)].astype(F32)
    halo.wait_recv()
    wide[:, pl.ds(0, HALO)] = hyena_buf[:, pl.ds(0, HALO)].astype(F32)
    feat_taps, inner_taps = feat.shape[0], inner.shape[0]

    def tile_lanes(mask):
        return jnp.concatenate([mask] * (channels // 128), axis=1)

    def featured(group, start, count, masks):
        result = None
        for tap in range(feat_taps):
            term = feat[tap, group][None, :] * wide[group, pl.ds(start - tap, count), :]
            if tap > 0:
                term = term * masks[tap]
            result = term if result is None else result + term
        return result

    def masks_of(start, count, taps):
        here = seg_col[pl.ds(start, count), :]
        return [None] + [
            tile_lanes((seg_col[pl.ds(start - tap, count), :] == here).astype(F32))
            for tap in range(1, taps)
        ]

    masks = masks_of(8, 8, feat_taps)
    product[pl.ds(8, 8), :] = featured(1, 8, 8, masks) * featured(2, 8, 8, masks)

    relays = [functools.partial(first_hop, 0, group) for group in range(1, last_group)]
    between = rows // 8 // (len(relays) + 1) if relays else rows
    for step, start in enumerate(range(HALO, HALO + rows, 8)):
        if step > 0 and step % between == 0 and relays:
            relays.pop(0)()
        masks = masks_of(start, 8, inner_taps)
        key_value = featured(1, start, 8, masks) * featured(2, start, 8, masks)
        product[pl.ds(start, 8), :] = key_value
        mixing = inner[0][None, :] * key_value
        for tap in range(1, inner_taps):
            mixing = mixing + inner[tap][None, :] * product[pl.ds(start - tap, 8), :] * masks[tap]
        gate_free[pl.ds(start - HALO, 8), :] = featured(0, start, 8, masks) * mixing

    for start in range(0, rows, 16):
        stream = (in_buf[pl.ds(start, 16), :].astype(F32) + gate_free[pl.ds(start, 16), :]).astype(BF16)
        stream_buf[pl.ds(start, 16), :] = stream
        stream = stream.astype(F32)
        square = stream * stream
        folded = square[:, 0:128]
        for lane in range(128, channels, 128):
            folded = folded + square[:, lane:lane + 128]
        total_col[pl.ds(start, 16), :] = folded
    store_s = pltpu.make_async_copy(stream_buf, stream_out, load_sem.at[0])
    store_s.start()

    padded = total_col.shape[0]
    if padded > rows:
        total_col[pl.ds(rows, padded - rows), :] = jnp.zeros((padded - rows, 128), F32)
    for start in range(0, padded, 128):
        turned = total_col[pl.ds(start, 128), :].T
        row = jnp.sum(turned, axis=0, keepdims=True)
        sums[tp, :, pl.ds(start, 128)] = jnp.broadcast_to(row, (8, 128))
    sum_copies = []
    for step in range(1, ring_tp):
        copy = pltpu.make_async_remote_copy(
            src_ref=sums.at[tp], dst_ref=sums.at[tp],
            send_sem=sum_send.at[step], recv_sem=sum_recv.at[step],
            device_id=(ctx, (tp + step) % ring_tp), device_id_type=MESH,
        )
        copy.start()
        sum_copies.append(copy)
    early = min(4, ring_z - 1)
    for copy in q_copies[:early]:
        copy.start()

    total = sums[tp]
    for copy in sum_copies:
        copy.wait_recv()
    for step in range(1, ring_tp):
        total = total + sums[(tp + step) % ring_tp]
    scale = lax.rsqrt(total / (channels * ring_tp) + EPSILON)
    for start in range(0, padded, 128):
        row = jnp.broadcast_to(scale[0:1, start:start + 128], (128, 128))
        total_col[pl.ds(start, 128), :] = row.T
    for start in range(0, rows, 16):
        norm = tile_lanes(total_col[pl.ds(start, 16), :])
        values[pl.ds(start, 16), :] = (stream_buf[pl.ds(start, 16), :].astype(F32) * norm).astype(BF16)

    for copy in v_copies:
        copy.start()
    own_v.start()
    if last_group > 0:
        first_hop(0, last_group)
    for group in range(len(groups)):
        second_hop(0, group)
    first_hop(1, 0)

    def query_columns(slot, carry):
        row_z = (z + jnp.where(slot % 2 == 1, (slot + 1) // 2, ring_z - slot // 2)) % ring_z
        begin = columns(row_z * RING_X + x)
        seg_query[slot] = turn_buf[pl.ds(begin, rows), :]
        return carry

    lax.fori_loop(1, ring_z, query_columns, 0)
    for copy in q_copies[early:]:
        copy.start()
    arrived(0)

    def tile_of(array, row_z):
        slot = slot_of((row_z - z + ring_z) % ring_z, ring_z)
        return array[slot].reshape(span, HEAD_DIM)

    def weigh(slot):
        row_z = z_at(offsets[slot])
        low = jnp.maximum(row_z - reach, 0)

        def score(index, carry):
            scores_buf[index - low] = lax.dot_general(
                q_all[slot], tile_of(k_all, index), (((1,), (1,)), ((), ())),
                preferred_element_type=F32,
            )
            return carry

        lax.fori_loop(low, row_z + 1, score, 0)

        def mask_tile(index, top, diagonal):
            documents = jnp.concatenate(
                [seg_buf[pl.ds(index * lane_rows + i, 1), :] for i in range(lane_rows)], axis=1
            ).astype(F32)
            tops = []
            for start in range(0, rows, CHUNK):
                here = jnp.concatenate([seg_query[slot, pl.ds(start, CHUNK), :]] * lane_rows, axis=1)
                allowed = here == documents
                if diagonal:
                    row_at = x * rows + start + lax.broadcasted_iota(jnp.int32, (CHUNK, span), 0)
                    allowed = allowed & (lax.broadcasted_iota(jnp.int32, (CHUNK, span), 1) <= row_at)
                scores = jnp.where(allowed, scores_buf[index - low, pl.ds(start, CHUNK), :], -BIG)
                scores_buf[index - low, pl.ds(start, CHUNK), :] = scores
                most_here = top[start:start + CHUNK]
                for lane in range(0, span, 128):
                    most_here = jnp.maximum(most_here, scores[:, lane:lane + 128])
                tops.append(most_here)
            return jnp.concatenate(tops, axis=0)

        top = lax.fori_loop(
            low, row_z, lambda index, top: mask_tile(index, top, False), jnp.full((rows, 128), -BIG, F32)
        )
        top = mask_tile(row_z, top, True)
        top = jnp.broadcast_to(jnp.max(top, axis=1, keepdims=True), (rows, 128))

        def term_tile(index, totals):
            parts = []
            for start in range(0, rows, CHUNK):
                total_here = totals[start:start + CHUNK]
                for lane in range(0, span, 128):
                    scores = scores_buf[index - low, pl.ds(start, CHUNK), lane:lane + 128]
                    terms = jnp.exp2((scores - top[start:start + CHUNK]) * factor)
                    total_here = total_here + terms
                    terms_buf[slot, index - low, pl.ds(start, CHUNK), lane:lane + 128] = terms.astype(BF16)
                parts.append(total_here)
            return jnp.concatenate(parts, axis=0)

        totals = lax.fori_loop(low, row_z + 1, term_tile, jnp.zeros((rows, 128), F32))
        inverse[slot] = jnp.broadcast_to(1.0 / jnp.sum(totals, axis=1, keepdims=True), (rows, 128))

    def add_up(slot):
        row_z = z_at(offsets[slot])
        low = jnp.maximum(row_z - reach, 0)
        summed[...] = jnp.zeros((rows, HEAD_DIM), F32)

        def add_tile(index, carry):
            summed[...] += jnp.dot(
                terms_buf[slot, index - low], tile_of(v_all, index), preferred_element_type=F32
            )
            return carry

        lax.fori_loop(low, row_z + 1, add_tile, 0)
        results[slot] = (summed[...] * inverse[slot]).astype(BF16)

    back_copies = []

    def give_back(slot):
        copy = pltpu.make_async_remote_copy(
            src_ref=results.at[slot], dst_ref=attended.at[:, head_cols(z)],
            send_sem=back_send.at[slot], recv_sem=back_recv.at[slot],
            device_id=(z_at(offsets[slot]) * RING_X + x, tp), device_id_type=MESH,
        )
        copy.start()
        back_copies.append(copy)

    relays = [functools.partial(first_hop, 1, group) for group in range(1, len(groups))]
    relays += [functools.partial(second_hop, 1, group) for group in range(len(groups))]
    own_q.wait()
    for slot in range(early + 1):
        if slot > 0:
            q_copies[slot - 1].wait_recv()
        weigh(slot)
        for _ in range(2):
            if relays:
                relays.pop(0)()
    for relay in relays:
        relay()
    for slot in range(early + 1, ring_z):
        q_copies[slot - 1].wait_recv()
        weigh(slot)
    arrived(1)
    for slot in list(range(1, ring_z)) + [0]:
        add_up(slot)
        if slot > 0:
            give_back(slot)
    own_o = pltpu.make_async_copy(results.at[0], attended.at[:, head_cols(z)], own_sem.at[0])
    own_o.start()
    own_o.wait()
    for slot in range(1, ring_z):
        pltpu.make_async_remote_copy(
            src_ref=results.at[slot], dst_ref=attended.at[:, head_cols(z_at(-offsets[slot]))],
            send_sem=back_send.at[slot], recv_sem=back_recv.at[slot],
            device_id=(z_at(offsets[slot]) * RING_X + x, tp), device_id_type=MESH,
        ).wait_recv()
    store_s.wait()
    halo.wait_send()
    for copy in sum_copies + k_copies + v_copies + q_copies + x_copies + back_copies:
        copy.wait_send()


ANY = pl.BlockSpec(memory_space=pl.ANY)
HBM = pl.BlockSpec(memory_space=pltpu.HBM)


def body(ring_ctx, ring_tp, most, hyena_in, stream_in, feat_filter, inner_filter, queries, key_vectors, segments):
    rows, channels = stream_in.shape
    ring_z = ring_ctx // RING_X
    tokens = segments.shape[0]
    hyena = jnp.transpose(hyena_in, (1, 0, 2))
    padded = -(-rows // 128) * 128
    span = RING_X * rows
    tiles = -(-most // span) + 1
    groups = 1 + ring_z // 2
    turned = 128 * (-(-rows // 128) + 1)
    dma = pltpu.SemaphoreType.DMA
    block = pltpu.VMEM((rows, channels), BF16)
    gathered = pltpu.VMEM((ring_z, RING_X, rows, HEAD_DIM), BF16)
    by_row = (ring_z, rows, HEAD_DIM)
    out = jax.ShapeDtypeStruct((rows, channels), BF16)
    return pl.pallas_call(
        functools.partial(mixer_kernel, ring_z, ring_tp, rows, most),
        name="mixer",
        out_shape=(out, out),
        in_specs=[HBM] * 7,
        out_specs=(ANY, ANY),
        scratch_shapes=[
            pltpu.VMEM((3, HALO + rows, channels), BF16),
            pltpu.VMEM((3, HALO + rows, channels), F32),
            pltpu.VMEM((HALO + rows, channels), F32),
            pltpu.VMEM((rows, channels), F32),
            block, block, block,
            pltpu.VMEM(feat_filter.shape, F32),
            pltpu.VMEM(inner_filter.shape, F32),
            pltpu.VMEM((tokens // 128, 128), jnp.int32),
            pltpu.VMEM((turned, 128), F32),
            pltpu.VMEM((HALO + rows, 128), F32),
            pltpu.VMEM((ring_z, rows, 128), F32),
            pltpu.VMEM((ring_tp, 8, padded), F32),
            pltpu.VMEM((padded, 128), F32),
            pltpu.VMEM(by_row, BF16),
            gathered, gathered,
            pltpu.VMEM((tiles, rows, span), F32),
            pltpu.VMEM((ring_z, tiles, rows, span), BF16),
            pltpu.VMEM(by_row, F32),
            pltpu.VMEM((rows, HEAD_DIM), F32),
            pltpu.VMEM(by_row, BF16),
            dma((5,)), dma((3,)), dma((2,)), dma((ring_tp,)), dma((ring_tp,)),
            dma((3, ring_z)), dma((3, ring_z)),
            dma((2, groups, 2)), dma((2, groups, 2)),
            dma((2, groups, 2)), dma((2, groups, 2)),
            dma((ring_z,)), dma((ring_z,)),
        ],
        compiler_params=pltpu.CompilerParams(
            collective_id=0, has_side_effects=True, vmem_limit_bytes=48 * 1024 * 1024
        ),
    )(*(
        pltpu.with_memory_space_constraint(value, pltpu.HBM)
        for value in (
            hyena, stream_in, feat_filter, inner_filter, queries, key_vectors,
            segments.reshape(tokens // 128, 128),
        )
    ))


def solution(mesh):
    in_specs = (
        P("ctx", None, "tp"),
        P("ctx", "tp"),
        P(None, None, "tp"),
        P(None, "tp"),
        P("ctx", "tp"),
        P("ctx", "tp"),
        P(),
    )
    out_specs = (P("ctx", "tp"), P("ctx", "tp"))

    def whole(*args):
        most = args[-1].shape[0] // 2
        mapped = jax.shard_map(
            functools.partial(body, mesh.shape["ctx"], mesh.shape["tp"], most),
            mesh=mesh, in_specs=in_specs, out_specs=out_specs, check_vma=False,
        )
        return mapped(*args)

    return whole
```

```python
import functools
import math

import jax
import jax.numpy as jnp
from jax import lax
from jax.experimental import pallas as pl
from jax.experimental.pallas import tpu as pltpu
from jax.sharding import PartitionSpec as P

HEAD_DIM = 128
HALO = 16
EPSILON = 1e-05
BIG = 1e30
CHUNK = 64
PRE_STEPS = 4
EARLY = 2
K_PUMPS = 3
V_PUMPS = (1, 1, 2, 2, 2, 2)
MESH = pl.DeviceIdType.MESH
F32 = jnp.float32
BF16 = jnp.bfloat16
RING_X = 4


def ring_offsets(count):
    offsets = [0]
    for distance in range(1, count // 2 + 1):
        offsets.append(distance)
        if distance != count - distance:
            offsets.append(-distance)
    return offsets


def slot_of(delta, count):
    ahead = jnp.maximum(2 * delta - 1, 0)
    return jnp.where(delta <= count // 2, ahead, 2 * (count - delta))


def mixer_kernel(
    ring_z, ring_tp, rows, most,
    hyena, stream_in, feat_in, inner_in, queries, keys, seg,
    stream_out, attended,
    hyena_buf, wide, product, gate_free, in_buf, stream_buf, values, feat, inner,
    seg_buf, turn_buf, seg_col, seg_query, sums, total_col,
    q_all, k_all, v_all, scores_buf, terms_buf, inverse, top_buf, summed, results,
    load_sem, own_sem, halo_sem, sum_send, sum_recv,
    z_send, z_recv, x_send, x_recv, far_send, far_recv, back_send, back_recv,
):
    ctx = lax.axis_index("ctx")
    tp = lax.axis_index("tp")
    z = ctx // RING_X
    x = ctx % RING_X
    ring_ctx = ring_z * RING_X
    channels = queries.shape[1]
    offsets = ring_offsets(ring_z)
    half = rows // 2
    right = (x + 1) % RING_X
    left = (x + RING_X - 1) % RING_X
    far = (x + 2) % RING_X
    right_id = (z * RING_X + right, tp)
    left_id = (z * RING_X + left, tp)
    next_ctx = (ctx + 1) % ring_ctx
    prev_ctx = (ctx + ring_ctx - 1) % ring_ctx
    span = RING_X * rows
    reach = -(-most // span)
    lane_rows = span // 128
    turns = turn_buf.shape[0] // 128
    factor = math.log2(math.e) / math.sqrt(HEAD_DIM)

    def z_at(offset):
        return (z + offset + ring_z) % ring_z

    def head_cols(index):
        return pl.ds(pl.multiple_of(index * HEAD_DIM, HEAD_DIM), HEAD_DIM)

    loads = [
        pltpu.make_async_copy(source, target, load_sem.at[index])
        for index, (source, target) in enumerate((
            (seg, seg_buf),
            (feat_in, feat),
            (inner_in, inner),
            (hyena, hyena_buf.at[:, pl.ds(HALO, rows)]),
            (stream_in, in_buf),
        ))
    ]
    own_k = pltpu.make_async_copy(keys.at[:, head_cols(z)], k_all.at[0, x], own_sem.at[0])
    own_q = pltpu.make_async_copy(queries.at[:, head_cols(z)], q_all.at[0], own_sem.at[1])

    barrier = pltpu.get_barrier_semaphore()
    partners = [(z_at(offset) * RING_X + x, tp) for offset in offsets[1:]]
    partners += [right_id, left_id, (next_ctx, tp), (prev_ctx, tp)]
    partners += [(ctx, (tp + step) % ring_tp) for step in range(1, ring_tp)]
    for partner in partners:
        pl.semaphore_signal(barrier, inc=1, device_id=partner, device_id_type=MESH)
    for load in loads:
        load.start()
    own_k.start()
    own_q.start()

    def columns(block):
        first = block * rows
        top_row = first // 128 - 1
        for turn in range(turns):
            row = seg_buf[pl.ds(jnp.maximum(top_row + turn, 0), 1), :].astype(F32)
            turn_buf[pl.ds(turn * 128, 128), :] = jnp.broadcast_to(row, (128, 128)).T
        return pl.multiple_of(first - top_row * 128, 16)

    loads[0].wait()
    start_at = columns(ctx)
    seg_col[...] = turn_buf[pl.ds(start_at - HALO, HALO + rows), :]
    seg_col[pl.ds(0, HALO), :] = jnp.where(ctx == 0, -1.0, seg_col[pl.ds(0, HALO), :])
    seg_query[0] = seg_col[pl.ds(HALO, rows), :]

    feat_taps, inner_taps = feat.shape[0], inner.shape[0]

    def tile_lanes(mask):
        return jnp.concatenate([mask] * (channels // 128), axis=1)

    def featured(group, start, count, masks):
        result = None
        for tap in range(feat_taps):
            term = feat[tap, group][None, :] * wide[group, pl.ds(start - tap, count), :]
            if tap > 0:
                term = term * masks[tap]
            result = term if result is None else result + term
        return result

    def masks_of(start, count, taps):
        here = seg_col[pl.ds(start, count), :]
        return [None] + [
            tile_lanes((seg_col[pl.ds(start - tap, count), :] == here).astype(F32))
            for tap in range(1, taps)
        ]

    def product_only(start):
        masks = masks_of(start, 8, feat_taps)
        product[pl.ds(start, 8), :] = featured(1, start, 8, masks) * featured(2, start, 8, masks)

    def convolve(start):
        masks = masks_of(start, 8, inner_taps)
        key_value = featured(1, start, 8, masks) * featured(2, start, 8, masks)
        product[pl.ds(start, 8), :] = key_value
        mixing = inner[0][None, :] * key_value
        for tap in range(1, inner_taps):
            mixing = mixing + inner[tap][None, :] * product[pl.ds(start - tap, 8), :] * masks[tap]
        gate_free[pl.ds(start - HALO, 8), :] = featured(0, start, 8, masks) * mixing

    inside = list(range(HALO + 16, HALO + rows, 8))
    before = min(PRE_STEPS, len(inside))
    for load in loads[1:]:
        load.wait()
    wide[:, pl.ds(HALO, rows)] = hyena_buf[:, pl.ds(HALO, rows)].astype(F32)
    product_only(HALO + 8)
    for start in inside[:before]:
        convolve(start)

    pl.semaphore_wait(barrier, len(partners))

    halo = pltpu.make_async_remote_copy(
        src_ref=hyena.at[:, pl.ds(rows - HALO, HALO)],
        dst_ref=hyena_buf.at[:, pl.ds(0, HALO)],
        send_sem=halo_sem.at[0], recv_sem=halo_sem.at[1],
        device_id=(next_ctx, tp), device_id_type=MESH,
    )
    halo.start()

    def z_copy(kind, slot, source, target):
        goal = z_at(-offsets[slot])
        return pltpu.make_async_remote_copy(
            src_ref=source.at[:, head_cols(goal)], dst_ref=target,
            send_sem=z_send.at[kind, slot], recv_sem=z_recv.at[kind, slot],
            device_id=(goal * RING_X + x, tp), device_id_type=MESH,
        )

    k_copies = [z_copy(0, slot, keys, k_all.at[slot, x]) for slot in range(1, ring_z)]
    for copy in k_copies:
        copy.start()
    v_copies = [z_copy(1, slot, values, v_all.at[slot, x]) for slot in range(1, ring_z)]
    own_v = pltpu.make_async_copy(values.at[:, head_cols(z)], v_all.at[0, x], own_sem.at[2])
    q_copies = [z_copy(2, slot, queries, q_all.at[slot]) for slot in range(1, ring_z)]

    groups = [(0, 1)] + [(lo, min(lo + 2, ring_z)) for lo in range(1, ring_z, 2)]
    last_group = len(groups) - 1
    x_copies = []

    def near(kind, group, way, array, source):
        lo, hi = groups[group]
        view = array.at[pl.ds(lo, hi - lo), source]
        return pltpu.make_async_remote_copy(
            src_ref=view, dst_ref=view,
            send_sem=x_send.at[kind, group, way], recv_sem=x_recv.at[kind, group, way],
            device_id=(right_id, left_id)[way], device_id_type=MESH,
        )

    def further(kind, group, way, array, source):
        lo, hi = groups[group]
        view = array.at[pl.ds(lo, hi - lo), source, pl.ds(way * half, half)]
        return pltpu.make_async_remote_copy(
            src_ref=view, dst_ref=view,
            send_sem=far_send.at[kind, group, way], recv_sem=far_recv.at[kind, group, way],
            device_id=(right_id, left_id)[way], device_id_type=MESH,
        )

    def first_hop(kind, group):
        array, copies, own = ((k_all, k_copies, own_k), (v_all, v_copies, own_v))[kind]
        lo, hi = groups[group]
        if lo == 0:
            own.wait()
        else:
            for slot in range(lo, hi):
                copies[slot - 1].wait_recv()
        for way in range(2):
            copy = near(kind, group, way, array, x)
            copy.start()
            x_copies.append(copy)

    def second_hop(kind, group):
        array = (k_all, v_all)[kind]
        for way in range(2):
            near(kind, group, way, array, (left, right)[way]).wait_recv()
            copy = further(kind, group, way, array, (left, right)[way])
            copy.start()
            x_copies.append(copy)

    def arrived(kind):
        for group in range(len(groups)):
            for way in range(2):
                further(kind, group, way, (k_all, v_all)[kind], far).wait_recv()

    first_hop(0, 0)

    for start in inside[before:]:
        convolve(start)
    waiting = [functools.partial(first_hop, 0, group) for group in range(1, len(groups))]

    def pump(count):
        for _ in range(min(count, len(waiting))):
            waiting.pop(0)()

    pump(1)
    halo.wait_recv()
    wide[:, pl.ds(0, HALO)] = hyena_buf[:, pl.ds(0, HALO)].astype(F32)
    product_only(8)
    convolve(HALO)
    convolve(HALO + 8)
    for start in range(0, rows, 16):
        stream = (in_buf[pl.ds(start, 16), :].astype(F32) + gate_free[pl.ds(start, 16), :]).astype(BF16)
        stream_buf[pl.ds(start, 16), :] = stream
        stream = stream.astype(F32)
        square = stream * stream
        folded = square[:, 0:128]
        for lane in range(128, channels, 128):
            folded = folded + square[:, lane:lane + 128]
        total_col[pl.ds(start, 16), :] = folded
    store_s = pltpu.make_async_copy(stream_buf, stream_out, load_sem.at[0])
    store_s.start()

    padded = total_col.shape[0]
    if padded > rows:
        total_col[pl.ds(rows, padded - rows), :] = jnp.zeros((padded - rows, 128), F32)
    for start in range(0, padded, 128):
        turned = total_col[pl.ds(start, 128), :].T
        row = jnp.sum(turned, axis=0, keepdims=True)
        sums[tp, :, pl.ds(start, 128)] = jnp.broadcast_to(row, (8, 128))
    sum_copies = []
    for step in range(1, ring_tp):
        copy = pltpu.make_async_remote_copy(
            src_ref=sums.at[tp], dst_ref=sums.at[tp],
            send_sem=sum_send.at[step], recv_sem=sum_recv.at[step],
            device_id=(ctx, (tp + step) % ring_tp), device_id_type=MESH,
        )
        copy.start()
        sum_copies.append(copy)
    early = min(EARLY, ring_z - 1)
    for copy in q_copies[:early]:
        copy.start()

    waiting[1:1] = [functools.partial(second_hop, 0, 0)]
    waiting[3:3] = [functools.partial(second_hop, 0, 1)]
    pump(K_PUMPS)
    total = sums[tp]
    for copy in sum_copies:
        copy.wait_recv()
    for step in range(1, ring_tp):
        total = total + sums[(tp + step) % ring_tp]
    scale = lax.rsqrt(total / (channels * ring_tp) + EPSILON)
    for start in range(0, padded, 128):
        row = jnp.broadcast_to(scale[0:1, start:start + 128], (128, 128))
        total_col[pl.ds(start, 128), :] = row.T
    for start in range(0, rows, 16):
        norm = tile_lanes(total_col[pl.ds(start, 16), :])
        values[pl.ds(start, 16), :] = (stream_buf[pl.ds(start, 16), :].astype(F32) * norm).astype(BF16)

    for copy in v_copies:
        copy.start()
    own_v.start()
    for copy in q_copies[early:]:
        copy.start()
    waiting += [functools.partial(second_hop, 0, group) for group in range(2, len(groups))]
    waiting += [functools.partial(first_hop, 1, 0)]
    pump(len(waiting))

    def query_columns(slot, carry):
        row_z = (z + jnp.where(slot % 2 == 1, (slot + 1) // 2, ring_z - slot // 2)) % ring_z
        begin = columns(row_z * RING_X + x)
        seg_query[slot] = turn_buf[pl.ds(begin, rows), :]
        return carry

    lax.fori_loop(1, ring_z, query_columns, 0)
    waiting += [functools.partial(first_hop, 1, group) for group in range(1, len(groups))]
    waiting += [functools.partial(second_hop, 1, group) for group in range(len(groups))]
    pump(1)
    arrived(0)

    def tile_of(array, row_z):
        slot = slot_of((row_z - z + ring_z) % ring_z, ring_z)
        return array[slot].reshape(span, HEAD_DIM)

    def weigh(slot):
        row_z = z_at(offsets[slot])
        low = jnp.maximum(row_z - reach, 0)

        def score(index, carry):
            scores_buf[index - low] = lax.dot_general(
                q_all[slot], tile_of(k_all, index), (((1,), (1,)), ((), ())),
                preferred_element_type=F32,
            )
            return carry

        @pl.when(row_z < reach)
        def _():
            lax.fori_loop(0, row_z + 1, score, 0)

        @pl.when(row_z >= reach)
        def _():
            for index in range(reach + 1):
                score(low + index, 0)

        def mask_tile(index, top, diagonal):
            documents = jnp.concatenate(
                [seg_buf[pl.ds(index * lane_rows + i, 1), :] for i in range(lane_rows)], axis=1
            ).astype(F32)
            tops = []
            for start in range(0, rows, CHUNK):
                here = jnp.concatenate([seg_query[slot, pl.ds(start, CHUNK), :]] * lane_rows, axis=1)
                allowed = here == documents
                if diagonal:
                    row_at = x * rows + start + lax.broadcasted_iota(jnp.int32, (CHUNK, span), 0)
                    allowed = allowed & (lax.broadcasted_iota(jnp.int32, (CHUNK, span), 1) <= row_at)
                scores = jnp.where(allowed, scores_buf[index - low, pl.ds(start, CHUNK), :], -BIG)
                scores_buf[index - low, pl.ds(start, CHUNK), :] = scores
                most_here = top[start:start + CHUNK]
                for lane in range(0, span, 128):
                    most_here = jnp.maximum(most_here, scores[:, lane:lane + 128])
                tops.append(most_here)
            return jnp.concatenate(tops, axis=0)

        def largest(top):
            top = mask_tile(row_z, top, True)
            top_buf[...] = jnp.broadcast_to(jnp.max(top, axis=1, keepdims=True), (rows, 128))

        @pl.when(row_z < reach)
        def _():
            largest(lax.fori_loop(
                0, row_z, lambda index, top: mask_tile(index, top, False),
                jnp.full((rows, 128), -BIG, F32),
            ))

        @pl.when(row_z >= reach)
        def _():
            top = jnp.full((rows, 128), -BIG, F32)
            for index in range(reach):
                top = mask_tile(low + index, top, False)
            largest(top)

        def term_tile(index, totals):
            parts = []
            for start in range(0, rows, CHUNK):
                total_here = totals[start:start + CHUNK]
                top = top_buf[pl.ds(start, CHUNK), :]
                for lane in range(0, span, 128):
                    scores = scores_buf[index, pl.ds(start, CHUNK), lane:lane + 128]
                    terms = jnp.exp2((scores - top) * factor)
                    total_here = total_here + terms
                    terms_buf[slot, index, pl.ds(start, CHUNK), lane:lane + 128] = terms.astype(BF16)
                parts.append(total_here)
            return jnp.concatenate(parts, axis=0)

        def divide_by(totals):
            inverse[slot] = jnp.broadcast_to(1.0 / jnp.sum(totals, axis=1, keepdims=True), (rows, 128))

        @pl.when(row_z < reach)
        def _():
            divide_by(lax.fori_loop(0, row_z + 1, term_tile, jnp.zeros((rows, 128), F32)))

        @pl.when(row_z >= reach)
        def _():
            totals = jnp.zeros((rows, 128), F32)
            for index in range(reach + 1):
                totals = term_tile(index, totals)
            divide_by(totals)

    def add_up(slot):
        row_z = z_at(offsets[slot])
        low = jnp.maximum(row_z - reach, 0)

        def add_tile(index, carry):
            summed[...] += jnp.dot(
                terms_buf[slot, index - low], tile_of(v_all, index), preferred_element_type=F32
            )
            return carry

        @pl.when(row_z < reach)
        def _():
            summed[...] = jnp.zeros((rows, HEAD_DIM), F32)
            lax.fori_loop(0, row_z + 1, add_tile, 0)

        @pl.when(row_z >= reach)
        def _():
            total = None
            for index in range(reach + 1):
                part = jnp.dot(
                    terms_buf[slot, index], tile_of(v_all, low + index), preferred_element_type=F32
                )
                total = part if total is None else total + part
            summed[...] = total

        results[slot] = (summed[...] * inverse[slot]).astype(BF16)

    back_copies = []

    def give_back(slot):
        copy = pltpu.make_async_remote_copy(
            src_ref=results.at[slot], dst_ref=attended.at[:, head_cols(z)],
            send_sem=back_send.at[slot], recv_sem=back_recv.at[slot],
            device_id=(z_at(offsets[slot]) * RING_X + x, tp), device_id_type=MESH,
        )
        copy.start()
        back_copies.append(copy)

    own_q.wait()
    for slot in range(ring_z):
        if slot > 0:
            q_copies[slot - 1].wait_recv()
        weigh(slot)
        pump(V_PUMPS[slot] if slot < len(V_PUMPS) else 0)
    pump(len(waiting))
    arrived(1)
    for slot in reversed(range(ring_z)):
        add_up(slot)
        if slot > 0:
            give_back(slot)
    own_o = pltpu.make_async_copy(results.at[0], attended.at[:, head_cols(z)], own_sem.at[0])
    own_o.start()
    own_o.wait()
    for slot in range(1, ring_z):
        pltpu.make_async_remote_copy(
            src_ref=results.at[slot], dst_ref=attended.at[:, head_cols(z_at(-offsets[slot]))],
            send_sem=back_send.at[slot], recv_sem=back_recv.at[slot],
            device_id=(z_at(offsets[slot]) * RING_X + x, tp), device_id_type=MESH,
        ).wait_recv()
    store_s.wait()
    halo.wait_send()
    for copy in sum_copies + k_copies + v_copies + q_copies + x_copies + back_copies:
        copy.wait_send()


ANY = pl.BlockSpec(memory_space=pl.ANY)
HBM = pl.BlockSpec(memory_space=pltpu.HBM)


def body(ring_ctx, ring_tp, most, hyena_in, stream_in, feat_filter, inner_filter, queries, key_vectors, segments):
    rows, channels = stream_in.shape
    ring_z = ring_ctx // RING_X
    tokens = segments.shape[0]
    hyena = jnp.transpose(hyena_in, (1, 0, 2))
    padded = -(-rows // 128) * 128
    span = RING_X * rows
    tiles = -(-most // span) + 1
    groups = 1 + ring_z // 2
    turned = 128 * (-(-rows // 128) + 1)
    dma = pltpu.SemaphoreType.DMA
    block = pltpu.VMEM((rows, channels), BF16)
    gathered = pltpu.VMEM((ring_z, RING_X, rows, HEAD_DIM), BF16)
    by_row = (ring_z, rows, HEAD_DIM)
    out = jax.ShapeDtypeStruct((rows, channels), BF16)
    return pl.pallas_call(
        functools.partial(mixer_kernel, ring_z, ring_tp, rows, most),
        name="mixer",
        out_shape=(out, out),
        in_specs=[HBM] * 7,
        out_specs=(ANY, ANY),
        scratch_shapes=[
            pltpu.VMEM((3, HALO + rows, channels), BF16),
            pltpu.VMEM((3, HALO + rows, channels), F32),
            pltpu.VMEM((HALO + rows, channels), F32),
            pltpu.VMEM((rows, channels), F32),
            block, block, block,
            pltpu.VMEM(feat_filter.shape, F32),
            pltpu.VMEM(inner_filter.shape, F32),
            pltpu.VMEM((tokens // 128, 128), jnp.int32),
            pltpu.VMEM((turned, 128), F32),
            pltpu.VMEM((HALO + rows, 128), F32),
            pltpu.VMEM((ring_z, rows, 128), F32),
            pltpu.VMEM((ring_tp, 8, padded), F32),
            pltpu.VMEM((padded, 128), F32),
            pltpu.VMEM(by_row, BF16),
            gathered, gathered,
            pltpu.VMEM((tiles, rows, span), F32),
            pltpu.VMEM((ring_z, tiles, rows, span), BF16),
            pltpu.VMEM(by_row, F32),
            pltpu.VMEM((rows, 128), F32),
            pltpu.VMEM((rows, HEAD_DIM), F32),
            pltpu.VMEM(by_row, BF16),
            dma((5,)), dma((3,)), dma((2,)), dma((ring_tp,)), dma((ring_tp,)),
            dma((3, ring_z)), dma((3, ring_z)),
            dma((2, groups, 2)), dma((2, groups, 2)),
            dma((2, groups, 2)), dma((2, groups, 2)),
            dma((ring_z,)), dma((ring_z,)),
        ],
        compiler_params=pltpu.CompilerParams(
            collective_id=0, has_side_effects=True, vmem_limit_bytes=48 * 1024 * 1024
        ),
    )(*(
        pltpu.with_memory_space_constraint(value, pltpu.HBM)
        for value in (
            hyena, stream_in, feat_filter, inner_filter, queries, key_vectors,
            segments.reshape(tokens // 128, 128),
        )
    ))


def solution(mesh):
    in_specs = (
        P("ctx", None, "tp"),
        P("ctx", "tp"),
        P(None, None, "tp"),
        P(None, "tp"),
        P("ctx", "tp"),
        P("ctx", "tp"),
        P(),
    )
    out_specs = (P("ctx", "tp"), P("ctx", "tp"))

    def whole(*args):
        most = args[-1].shape[0] // 2
        mapped = jax.shard_map(
            functools.partial(body, mesh.shape["ctx"], mesh.shape["tp"], most),
            mesh=mesh, in_specs=in_specs, out_specs=out_specs, check_vma=False,
        )
        return mapped(*args)

    return whole
```

```python
import functools
import math

import jax
import jax.numpy as jnp
from jax import lax
from jax.experimental import pallas as pl
from jax.experimental.pallas import tpu as pltpu
from jax.sharding import PartitionSpec as P

HEAD_DIM = 128
HALO = 16
EPSILON = 1e-05
BIG = 1e30
CHUNK = 64
PRE_STEPS = 4
EARLY = 2
K_PUMPS = 3
V_PUMPS = ((0, 1), (1, 1), (1, 1), (1, 1), (0, 1))
MESH = pl.DeviceIdType.MESH
F32 = jnp.float32
BF16 = jnp.bfloat16
RING_X = 4


def ring_offsets(count):
    offsets = [0]
    for distance in range(1, count // 2 + 1):
        offsets.append(distance)
        if distance != count - distance:
            offsets.append(-distance)
    return offsets


def slot_of(delta, count):
    ahead = jnp.maximum(2 * delta - 1, 0)
    return jnp.where(delta <= count // 2, ahead, 2 * (count - delta))


def mixer_kernel(
    ring_z, ring_tp, rows, most,
    hyena, stream_in, feat_in, inner_in, queries, keys, seg,
    stream_out, attended,
    hyena_buf, wide, product, gate_free, in_buf, stream_buf, values, feat, inner,
    seg_buf, turn_buf, seg_col, seg_query, sums, total_col,
    q_all, k_all, v_all, scores_buf, terms_buf, inverse, top_buf, summed, results,
    load_sem, own_sem, halo_sem, sum_send, sum_recv,
    z_send, z_recv, x_send, x_recv, far_send, far_recv, back_send, back_recv,
):
    ctx = lax.axis_index("ctx")
    tp = lax.axis_index("tp")
    z = ctx // RING_X
    x = ctx % RING_X
    ring_ctx = ring_z * RING_X
    channels = queries.shape[1]
    offsets = ring_offsets(ring_z)
    half = rows // 2
    right = (x + 1) % RING_X
    left = (x + RING_X - 1) % RING_X
    far = (x + 2) % RING_X
    right_id = (z * RING_X + right, tp)
    left_id = (z * RING_X + left, tp)
    next_ctx = (ctx + 1) % ring_ctx
    prev_ctx = (ctx + ring_ctx - 1) % ring_ctx
    span = RING_X * rows
    reach = -(-most // span)
    lane_rows = span // 128
    turns = turn_buf.shape[0] // 128
    factor = math.log2(math.e) / math.sqrt(HEAD_DIM)

    def z_at(offset):
        return (z + offset + ring_z) % ring_z

    def head_cols(index):
        return pl.ds(pl.multiple_of(index * HEAD_DIM, HEAD_DIM), HEAD_DIM)

    loads = [
        pltpu.make_async_copy(source, target, load_sem.at[index])
        for index, (source, target) in enumerate((
            (seg, seg_buf),
            (feat_in, feat),
            (inner_in, inner),
            (hyena, hyena_buf.at[:, pl.ds(HALO, rows)]),
            (stream_in, in_buf),
        ))
    ]
    own_k = pltpu.make_async_copy(keys.at[:, head_cols(z)], k_all.at[0, x], own_sem.at[0])
    own_q = pltpu.make_async_copy(queries.at[:, head_cols(z)], q_all.at[0], own_sem.at[1])

    barrier = pltpu.get_barrier_semaphore()
    partners = [(z_at(offset) * RING_X + x, tp) for offset in offsets[1:]]
    partners += [right_id, left_id, (next_ctx, tp), (prev_ctx, tp)]
    partners += [(ctx, (tp + step) % ring_tp) for step in range(1, ring_tp)]
    for partner in partners:
        pl.semaphore_signal(barrier, inc=1, device_id=partner, device_id_type=MESH)
    for load in loads:
        load.start()
    own_k.start()
    own_q.start()

    def columns(block):
        first = block * rows
        top_row = first // 128 - 1
        for turn in range(turns):
            row = seg_buf[pl.ds(jnp.maximum(top_row + turn, 0), 1), :].astype(F32)
            turn_buf[pl.ds(turn * 128, 128), :] = jnp.broadcast_to(row, (128, 128)).T
        return pl.multiple_of(first - top_row * 128, 16)

    loads[0].wait()
    start_at = columns(ctx)
    seg_col[...] = turn_buf[pl.ds(start_at - HALO, HALO + rows), :]
    seg_col[pl.ds(0, HALO), :] = jnp.where(ctx == 0, -1.0, seg_col[pl.ds(0, HALO), :])
    seg_query[0] = seg_col[pl.ds(HALO, rows), :]

    feat_taps, inner_taps = feat.shape[0], inner.shape[0]

    def tile_lanes(mask):
        return jnp.concatenate([mask] * (channels // 128), axis=1)

    def featured(group, start, count, masks):
        result = None
        for tap in range(feat_taps):
            term = feat[tap, group][None, :] * wide[group, pl.ds(start - tap, count), :]
            if tap > 0:
                term = term * masks[tap]
            result = term if result is None else result + term
        return result

    def masks_of(start, count, taps):
        here = seg_col[pl.ds(start, count), :]
        return [None] + [
            tile_lanes((seg_col[pl.ds(start - tap, count), :] == here).astype(F32))
            for tap in range(1, taps)
        ]

    def product_only(start):
        masks = masks_of(start, 8, feat_taps)
        product[pl.ds(start, 8), :] = featured(1, start, 8, masks) * featured(2, start, 8, masks)

    def convolve(start):
        masks = masks_of(start, 8, inner_taps)
        key_value = featured(1, start, 8, masks) * featured(2, start, 8, masks)
        product[pl.ds(start, 8), :] = key_value
        mixing = inner[0][None, :] * key_value
        for tap in range(1, inner_taps):
            mixing = mixing + inner[tap][None, :] * product[pl.ds(start - tap, 8), :] * masks[tap]
        gate_free[pl.ds(start - HALO, 8), :] = featured(0, start, 8, masks) * mixing

    inside = list(range(HALO + 16, HALO + rows, 8))
    before = min(PRE_STEPS, len(inside))
    for load in loads[1:]:
        load.wait()
    wide[:, pl.ds(HALO, rows)] = hyena_buf[:, pl.ds(HALO, rows)].astype(F32)
    product_only(HALO + 8)
    for start in inside[:before]:
        convolve(start)

    pl.semaphore_wait(barrier, len(partners))

    halo = pltpu.make_async_remote_copy(
        src_ref=hyena.at[:, pl.ds(rows - HALO, HALO)],
        dst_ref=hyena_buf.at[:, pl.ds(0, HALO)],
        send_sem=halo_sem.at[0], recv_sem=halo_sem.at[1],
        device_id=(next_ctx, tp), device_id_type=MESH,
    )
    halo.start()

    def z_copy(kind, slot, source, target):
        goal = z_at(-offsets[slot])
        return pltpu.make_async_remote_copy(
            src_ref=source.at[:, head_cols(goal)], dst_ref=target,
            send_sem=z_send.at[kind, slot], recv_sem=z_recv.at[kind, slot],
            device_id=(goal * RING_X + x, tp), device_id_type=MESH,
        )

    k_copies = [z_copy(0, slot, keys, k_all.at[slot, x]) for slot in range(1, ring_z)]
    for copy in k_copies:
        copy.start()
    v_copies = [z_copy(1, slot, values, v_all.at[slot, x]) for slot in range(1, ring_z)]
    own_v = pltpu.make_async_copy(values.at[:, head_cols(z)], v_all.at[0, x], own_sem.at[2])
    q_copies = [z_copy(2, slot, queries, q_all.at[slot]) for slot in range(1, ring_z)]

    groups = [(0, 1)] + [(lo, min(lo + 2, ring_z)) for lo in range(1, ring_z, 2)]
    last_group = len(groups) - 1
    x_copies = []

    def near(kind, group, way, array, source):
        lo, hi = groups[group]
        view = array.at[pl.ds(lo, hi - lo), source]
        return pltpu.make_async_remote_copy(
            src_ref=view, dst_ref=view,
            send_sem=x_send.at[kind, group, way], recv_sem=x_recv.at[kind, group, way],
            device_id=(right_id, left_id)[way], device_id_type=MESH,
        )

    def further(kind, group, way, array, source):
        lo, hi = groups[group]
        view = array.at[pl.ds(lo, hi - lo), source, pl.ds(way * half, half)]
        return pltpu.make_async_remote_copy(
            src_ref=view, dst_ref=view,
            send_sem=far_send.at[kind, group, way], recv_sem=far_recv.at[kind, group, way],
            device_id=(right_id, left_id)[way], device_id_type=MESH,
        )

    def first_hop(kind, group):
        array, copies, own = ((k_all, k_copies, own_k), (v_all, v_copies, own_v))[kind]
        lo, hi = groups[group]
        if lo == 0:
            own.wait()
        else:
            for slot in range(lo, hi):
                copies[slot - 1].wait_recv()
        for way in range(2):
            copy = near(kind, group, way, array, x)
            copy.start()
            x_copies.append(copy)

    def second_hop(kind, group):
        array = (k_all, v_all)[kind]
        for way in range(2):
            near(kind, group, way, array, (left, right)[way]).wait_recv()
            copy = further(kind, group, way, array, (left, right)[way])
            copy.start()
            x_copies.append(copy)

    def arrived(kind):
        for group in range(len(groups)):
            for way in range(2):
                further(kind, group, way, (k_all, v_all)[kind], far).wait_recv()

    first_hop(0, 0)

    for start in inside[before:]:
        convolve(start)
    waiting = [functools.partial(first_hop, 0, group) for group in range(1, len(groups))]

    def pump(count):
        for _ in range(min(count, len(waiting))):
            waiting.pop(0)()

    pump(1)
    halo.wait_recv()
    wide[:, pl.ds(0, HALO)] = hyena_buf[:, pl.ds(0, HALO)].astype(F32)
    product_only(8)
    convolve(HALO)
    convolve(HALO + 8)
    for start in range(0, rows, 16):
        stream = (in_buf[pl.ds(start, 16), :].astype(F32) + gate_free[pl.ds(start, 16), :]).astype(BF16)
        stream_buf[pl.ds(start, 16), :] = stream
        stream = stream.astype(F32)
        square = stream * stream
        folded = square[:, 0:128]
        for lane in range(128, channels, 128):
            folded = folded + square[:, lane:lane + 128]
        total_col[pl.ds(start, 16), :] = folded
    store_s = pltpu.make_async_copy(stream_buf, stream_out, load_sem.at[0])
    store_s.start()

    padded = total_col.shape[0]
    if padded > rows:
        total_col[pl.ds(rows, padded - rows), :] = jnp.zeros((padded - rows, 128), F32)
    for start in range(0, padded, 128):
        turned = total_col[pl.ds(start, 128), :].T
        row = jnp.sum(turned, axis=0, keepdims=True)
        sums[tp, :, pl.ds(start, 128)] = jnp.broadcast_to(row, (8, 128))
    sum_copies = []
    for step in range(1, ring_tp):
        copy = pltpu.make_async_remote_copy(
            src_ref=sums.at[tp], dst_ref=sums.at[tp],
            send_sem=sum_send.at[step], recv_sem=sum_recv.at[step],
            device_id=(ctx, (tp + step) % ring_tp), device_id_type=MESH,
        )
        copy.start()
        sum_copies.append(copy)
    early = min(EARLY, ring_z - 1)
    for copy in q_copies[:early]:
        copy.start()

    waiting[1:1] = [functools.partial(second_hop, 0, 0)]
    waiting[3:3] = [functools.partial(second_hop, 0, 1)]
    pump(K_PUMPS)

    def query_columns(slot, carry):
        row_z = (z + jnp.where(slot % 2 == 1, (slot + 1) // 2, ring_z - slot // 2)) % ring_z
        begin = columns(row_z * RING_X + x)
        seg_query[slot] = turn_buf[pl.ds(begin, rows), :]
        return carry

    lax.fori_loop(1, ring_z, query_columns, 0)
    total = sums[tp]
    for copy in sum_copies:
        copy.wait_recv()
    for step in range(1, ring_tp):
        total = total + sums[(tp + step) % ring_tp]
    scale = lax.rsqrt(total / (channels * ring_tp) + EPSILON)
    for start in range(0, padded, 128):
        row = jnp.broadcast_to(scale[0:1, start:start + 128], (128, 128))
        total_col[pl.ds(start, 128), :] = row.T
    for start in range(0, rows, 16):
        norm = tile_lanes(total_col[pl.ds(start, 16), :])
        values[pl.ds(start, 16), :] = (stream_buf[pl.ds(start, 16), :].astype(F32) * norm).astype(BF16)

    for copy in v_copies:
        copy.start()
    own_v.start()
    for copy in q_copies[early:]:
        copy.start()
    waiting += [functools.partial(second_hop, 0, group) for group in range(2, len(groups))]
    waiting += [functools.partial(first_hop, 1, 0)]
    pump(len(waiting))

    for group in range(1, len(groups) + 2):
        if group < len(groups):
            waiting.append(functools.partial(first_hop, 1, group))
        if group >= 2:
            waiting.append(functools.partial(second_hop, 1, group - 2))
    pump(1)
    arrived(0)

    def tile_of(array, row_z):
        slot = slot_of((row_z - z + ring_z) % ring_z, ring_z)
        return array[slot].reshape(span, HEAD_DIM)

    def weigh(slot, relays):
        row_z = z_at(offsets[slot])
        low = jnp.maximum(row_z - reach, 0)

        def score(index, carry):
            scores_buf[index - low] = lax.dot_general(
                q_all[slot], tile_of(k_all, index), (((1,), (1,)), ((), ())),
                preferred_element_type=F32,
            )
            return carry

        @pl.when(row_z < reach)
        def _():
            lax.fori_loop(0, row_z + 1, score, 0)

        @pl.when(row_z >= reach)
        def _():
            for index in range(reach + 1):
                score(low + index, 0)

        pump(relays)

        def mask_tile(index, top, diagonal):
            documents = jnp.concatenate(
                [seg_buf[pl.ds(index * lane_rows + i, 1), :] for i in range(lane_rows)], axis=1
            ).astype(F32)
            tops = []
            for start in range(0, rows, CHUNK):
                here = jnp.concatenate([seg_query[slot, pl.ds(start, CHUNK), :]] * lane_rows, axis=1)
                allowed = here == documents
                if diagonal:
                    row_at = x * rows + start + lax.broadcasted_iota(jnp.int32, (CHUNK, span), 0)
                    allowed = allowed & (lax.broadcasted_iota(jnp.int32, (CHUNK, span), 1) <= row_at)
                scores = jnp.where(allowed, scores_buf[index - low, pl.ds(start, CHUNK), :], -BIG)
                scores_buf[index - low, pl.ds(start, CHUNK), :] = scores
                most_here = top[start:start + CHUNK]
                for lane in range(0, span, 128):
                    most_here = jnp.maximum(most_here, scores[:, lane:lane + 128])
                tops.append(most_here)
            return jnp.concatenate(tops, axis=0)

        def largest(top):
            top = mask_tile(row_z, top, True)
            top_buf[...] = jnp.broadcast_to(jnp.max(top, axis=1, keepdims=True), (rows, 128))

        @pl.when(row_z < reach)
        def _():
            largest(lax.fori_loop(
                0, row_z, lambda index, top: mask_tile(index, top, False),
                jnp.full((rows, 128), -BIG, F32),
            ))

        @pl.when(row_z >= reach)
        def _():
            top = jnp.full((rows, 128), -BIG, F32)
            for index in range(reach):
                top = mask_tile(low + index, top, False)
            largest(top)

        def term_tile(index, totals):
            parts = []
            for start in range(0, rows, CHUNK):
                total_here = totals[start:start + CHUNK]
                top = top_buf[pl.ds(start, CHUNK), :]
                for lane in range(0, span, 128):
                    scores = scores_buf[index, pl.ds(start, CHUNK), lane:lane + 128]
                    terms = jnp.exp2((scores - top) * factor)
                    total_here = total_here + terms
                    terms_buf[slot, index, pl.ds(start, CHUNK), lane:lane + 128] = terms.astype(BF16)
                parts.append(total_here)
            return jnp.concatenate(parts, axis=0)

        def divide_by(totals):
            inverse[slot] = jnp.broadcast_to(1.0 / jnp.sum(totals, axis=1, keepdims=True), (rows, 128))

        @pl.when(row_z < reach)
        def _():
            divide_by(lax.fori_loop(0, row_z + 1, term_tile, jnp.zeros((rows, 128), F32)))

        @pl.when(row_z >= reach)
        def _():
            totals = jnp.zeros((rows, 128), F32)
            for index in range(reach + 1):
                totals = term_tile(index, totals)
            divide_by(totals)

    def add_up(slot):
        row_z = z_at(offsets[slot])
        low = jnp.maximum(row_z - reach, 0)

        def add_tile(index, carry):
            summed[...] += jnp.dot(
                terms_buf[slot, index - low], tile_of(v_all, index), preferred_element_type=F32
            )
            return carry

        @pl.when(row_z < reach)
        def _():
            summed[...] = jnp.zeros((rows, HEAD_DIM), F32)
            lax.fori_loop(0, row_z + 1, add_tile, 0)

        @pl.when(row_z >= reach)
        def _():
            total = None
            for index in range(reach + 1):
                part = jnp.dot(
                    terms_buf[slot, index], tile_of(v_all, low + index), preferred_element_type=F32
                )
                total = part if total is None else total + part
            summed[...] = total

        results[slot] = (summed[...] * inverse[slot]).astype(BF16)

    back_copies = []

    def give_back(slot):
        copy = pltpu.make_async_remote_copy(
            src_ref=results.at[slot], dst_ref=attended.at[:, head_cols(z)],
            send_sem=back_send.at[slot], recv_sem=back_recv.at[slot],
            device_id=(z_at(offsets[slot]) * RING_X + x, tp), device_id_type=MESH,
        )
        copy.start()
        back_copies.append(copy)

    own_q.wait()
    for slot in range(ring_z):
        if slot > 0:
            q_copies[slot - 1].wait_recv()
        inside_it, after_it = V_PUMPS[slot] if slot < len(V_PUMPS) else (0, 0)
        weigh(slot, inside_it)
        pump(after_it)
    pump(len(waiting))
    arrived(1)
    for slot in reversed(range(ring_z)):
        add_up(slot)
        if slot > 0:
            give_back(slot)
    own_o = pltpu.make_async_copy(results.at[0], attended.at[:, head_cols(z)], own_sem.at[0])
    own_o.start()
    own_o.wait()
    for slot in range(1, ring_z):
        pltpu.make_async_remote_copy(
            src_ref=results.at[slot], dst_ref=attended.at[:, head_cols(z_at(-offsets[slot]))],
            send_sem=back_send.at[slot], recv_sem=back_recv.at[slot],
            device_id=(z_at(offsets[slot]) * RING_X + x, tp), device_id_type=MESH,
        ).wait_recv()
    store_s.wait()
    halo.wait_send()
    for copy in sum_copies + k_copies + v_copies + q_copies + x_copies + back_copies:
        copy.wait_send()


def place_kernel(stream_from, attended_from, stream, attended, sem):
    copies = [
        pltpu.make_async_copy(stream_from, stream, sem.at[0]),
        pltpu.make_async_copy(attended_from, attended, sem.at[1]),
    ]
    for copy in copies:
        copy.start()
    for copy in copies:
        copy.wait()


ANY = pl.BlockSpec(memory_space=pl.ANY)
HBM = pl.BlockSpec(memory_space=pltpu.HBM)


def body(ring_ctx, ring_tp, most, hyena_in, stream_in, feat_filter, inner_filter, queries, key_vectors, segments):
    rows, channels = stream_in.shape
    ring_z = ring_ctx // RING_X
    tokens = segments.shape[0]
    hyena = jnp.transpose(hyena_in, (1, 0, 2))
    padded = -(-rows // 128) * 128
    span = RING_X * rows
    tiles = -(-most // span) + 1
    groups = 1 + ring_z // 2
    turned = 128 * (-(-rows // 128) + 1)
    dma = pltpu.SemaphoreType.DMA
    block = pltpu.VMEM((rows, channels), BF16)
    gathered = pltpu.VMEM((ring_z, RING_X, rows, HEAD_DIM), BF16)
    by_row = (ring_z, rows, HEAD_DIM)
    out = jax.ShapeDtypeStruct((rows, channels), BF16)
    results = pl.pallas_call(
        functools.partial(mixer_kernel, ring_z, ring_tp, rows, most),
        name="mixer",
        out_shape=(out, out),
        in_specs=[HBM] * 7,
        out_specs=(ANY, ANY),
        scratch_shapes=[
            pltpu.VMEM((3, HALO + rows, channels), BF16),
            pltpu.VMEM((3, HALO + rows, channels), F32),
            pltpu.VMEM((HALO + rows, channels), F32),
            pltpu.VMEM((rows, channels), F32),
            block, block, block,
            pltpu.VMEM(feat_filter.shape, F32),
            pltpu.VMEM(inner_filter.shape, F32),
            pltpu.VMEM((tokens // 128, 128), jnp.int32),
            pltpu.VMEM((turned, 128), F32),
            pltpu.VMEM((HALO + rows, 128), F32),
            pltpu.VMEM((ring_z, rows, 128), F32),
            pltpu.VMEM((ring_tp, 8, padded), F32),
            pltpu.VMEM((padded, 128), F32),
            pltpu.VMEM(by_row, BF16),
            gathered, gathered,
            pltpu.VMEM((tiles, rows, span), F32),
            pltpu.VMEM((ring_z, tiles, rows, span), BF16),
            pltpu.VMEM(by_row, F32),
            pltpu.VMEM((rows, 128), F32),
            pltpu.VMEM((rows, HEAD_DIM), F32),
            pltpu.VMEM(by_row, BF16),
            dma((5,)), dma((3,)), dma((2,)), dma((ring_tp,)), dma((ring_tp,)),
            dma((3, ring_z)), dma((3, ring_z)),
            dma((2, groups, 2)), dma((2, groups, 2)),
            dma((2, groups, 2)), dma((2, groups, 2)),
            dma((ring_z,)), dma((ring_z,)),
        ],
        compiler_params=pltpu.CompilerParams(
            collective_id=0, has_side_effects=True, vmem_limit_bytes=48 * 1024 * 1024
        ),
    )(*(
        pltpu.with_memory_space_constraint(value, pltpu.HBM)
        for value in (
            hyena, stream_in, feat_filter, inner_filter, queries, key_vectors,
            segments.reshape(tokens // 128, 128),
        )
    ))
    return pl.pallas_call(
        place_kernel,
        name="place",
        out_shape=(out, out),
        in_specs=[ANY] * 2,
        out_specs=(ANY, ANY),
        scratch_shapes=[dma((2,))],
        compiler_params=pltpu.CompilerParams(vmem_limit_bytes=48 * 1024 * 1024),
    )(*results)


def solution(mesh):
    in_specs = (
        P("ctx", None, "tp"),
        P("ctx", "tp"),
        P(None, None, "tp"),
        P(None, "tp"),
        P("ctx", "tp"),
        P("ctx", "tp"),
        P(),
    )
    out_specs = (P("ctx", "tp"), P("ctx", "tp"))

    def whole(*args):
        most = args[-1].shape[0] // 2
        mapped = jax.shard_map(
            functools.partial(body, mesh.shape["ctx"], mesh.shape["tp"], most),
            mesh=mesh, in_specs=in_specs, out_specs=out_specs, check_vma=False,
        )
        return mapped(*args)

    return whole
```

```python
import functools
import math

import jax
import jax.numpy as jnp
from jax import lax
from jax.experimental import pallas as pl
from jax.experimental.pallas import tpu as pltpu
from jax.sharding import PartitionSpec as P

HEAD_DIM = 128
HALO = 16
EPSILON = 1e-05
BIG = 1e30
CHUNK = 64
PRE_STEPS = 4
EARLY = 2
K_PUMPS = 2
V_PUMPS = ((0, 1), (1, 1), (1, 1), (1, 1), (0, 1))
MESH = pl.DeviceIdType.MESH
F32 = jnp.float32
BF16 = jnp.bfloat16
RING_X = 4


def ring_offsets(count):
    offsets = [0]
    for distance in range(1, count // 2 + 1):
        offsets.append(distance)
        if distance != count - distance:
            offsets.append(-distance)
    return offsets


def slot_of(delta, count):
    ahead = jnp.maximum(2 * delta - 1, 0)
    return jnp.where(delta <= count // 2, ahead, 2 * (count - delta))


def mixer_kernel(
    ring_z, ring_tp, rows, most,
    hyena, stream_in, feat_in, inner_in, queries, keys, seg,
    stream_out, attended,
    hyena_buf, wide, product, gate_free, in_buf, stream_buf, values, feat, inner,
    seg_buf, turn_buf, seg_col, seg_query, sums, total_col,
    q_all, k_all, v_all, scores_buf, terms_buf, inverse, top_buf, summed, results,
    load_sem, own_sem, halo_sem, sum_send, sum_recv,
    z_send, z_recv, x_send, x_recv, far_send, far_recv, back_send, back_recv,
):
    ctx = lax.axis_index("ctx")
    tp = lax.axis_index("tp")
    z = ctx // RING_X
    x = ctx % RING_X
    ring_ctx = ring_z * RING_X
    channels = queries.shape[1]
    offsets = ring_offsets(ring_z)
    half = rows // 2
    right = (x + 1) % RING_X
    left = (x + RING_X - 1) % RING_X
    far = (x + 2) % RING_X
    right_id = (z * RING_X + right, tp)
    left_id = (z * RING_X + left, tp)
    next_ctx = (ctx + 1) % ring_ctx
    prev_ctx = (ctx + ring_ctx - 1) % ring_ctx
    span = RING_X * rows
    reach = -(-most // span)
    lane_rows = span // 128
    turns = turn_buf.shape[0] // 128
    factor = math.log2(math.e) / math.sqrt(HEAD_DIM)

    def z_at(offset):
        return (z + offset + ring_z) % ring_z

    def head_cols(index):
        return pl.ds(pl.multiple_of(index * HEAD_DIM, HEAD_DIM), HEAD_DIM)

    loads = [
        pltpu.make_async_copy(source, target, load_sem.at[index])
        for index, (source, target) in enumerate((
            (seg, seg_buf),
            (feat_in, feat),
            (inner_in, inner),
            (hyena, hyena_buf.at[:, pl.ds(HALO, rows)]),
            (stream_in, in_buf),
        ))
    ]
    own_k = pltpu.make_async_copy(keys.at[:, head_cols(z)], k_all.at[0, x], own_sem.at[0])
    own_q = pltpu.make_async_copy(queries.at[:, head_cols(z)], q_all.at[0], own_sem.at[1])

    barrier = pltpu.get_barrier_semaphore()
    partners = [(z_at(offset) * RING_X + x, tp) for offset in offsets[1:]]
    partners += [right_id, left_id, (next_ctx, tp), (prev_ctx, tp)]
    partners += [(ctx, (tp + step) % ring_tp) for step in range(1, ring_tp)]
    for partner in partners:
        pl.semaphore_signal(barrier, inc=1, device_id=partner, device_id_type=MESH)
    for load in loads:
        load.start()
    own_k.start()
    own_q.start()

    def columns(block):
        first = block * rows
        top_row = first // 128 - 1
        for turn in range(turns):
            row = seg_buf[pl.ds(jnp.maximum(top_row + turn, 0), 1), :].astype(F32)
            turn_buf[pl.ds(turn * 128, 128), :] = jnp.broadcast_to(row, (128, 128)).T
        return pl.multiple_of(first - top_row * 128, 16)

    loads[0].wait()
    start_at = columns(ctx)
    seg_col[...] = turn_buf[pl.ds(start_at - HALO, HALO + rows), :]
    seg_col[pl.ds(0, HALO), :] = jnp.where(ctx == 0, -1.0, seg_col[pl.ds(0, HALO), :])
    seg_query[0] = seg_col[pl.ds(HALO, rows), :]

    feat_taps, inner_taps = feat.shape[0], inner.shape[0]

    def tile_lanes(mask):
        return jnp.concatenate([mask] * (channels // 128), axis=1)

    def featured(group, start, count, masks):
        result = None
        for tap in range(feat_taps):
            term = feat[tap, group][None, :] * wide[group, pl.ds(start - tap, count), :]
            if tap > 0:
                term = term * masks[tap]
            result = term if result is None else result + term
        return result

    def masks_of(start, count, taps):
        here = seg_col[pl.ds(start, count), :]
        return [None] + [
            tile_lanes((seg_col[pl.ds(start - tap, count), :] == here).astype(F32))
            for tap in range(1, taps)
        ]

    def product_only(start):
        masks = masks_of(start, 8, feat_taps)
        product[pl.ds(start, 8), :] = featured(1, start, 8, masks) * featured(2, start, 8, masks)

    def convolve(start):
        masks = masks_of(start, 8, inner_taps)
        key_value = featured(1, start, 8, masks) * featured(2, start, 8, masks)
        product[pl.ds(start, 8), :] = key_value
        mixing = inner[0][None, :] * key_value
        for tap in range(1, inner_taps):
            mixing = mixing + inner[tap][None, :] * product[pl.ds(start - tap, 8), :] * masks[tap]
        gate_free[pl.ds(start - HALO, 8), :] = featured(0, start, 8, masks) * mixing

    inside = list(range(HALO + 16, HALO + rows, 8))
    before = min(PRE_STEPS, len(inside))
    for load in loads[1:]:
        load.wait()
    wide[:, pl.ds(HALO, rows)] = hyena_buf[:, pl.ds(HALO, rows)].astype(F32)
    product_only(HALO + 8)
    for start in inside[:before]:
        convolve(start)

    pl.semaphore_wait(barrier, len(partners))

    halo = pltpu.make_async_remote_copy(
        src_ref=hyena.at[:, pl.ds(rows - HALO, HALO)],
        dst_ref=hyena_buf.at[:, pl.ds(0, HALO)],
        send_sem=halo_sem.at[0], recv_sem=halo_sem.at[1],
        device_id=(next_ctx, tp), device_id_type=MESH,
    )
    halo.start()

    def z_copy(kind, slot, source, target):
        goal = z_at(-offsets[slot])
        return pltpu.make_async_remote_copy(
            src_ref=source.at[:, head_cols(goal)], dst_ref=target,
            send_sem=z_send.at[kind, slot], recv_sem=z_recv.at[kind, slot],
            device_id=(goal * RING_X + x, tp), device_id_type=MESH,
        )

    k_copies = [z_copy(0, slot, keys, k_all.at[slot, x]) for slot in range(1, ring_z)]
    for copy in k_copies:
        copy.start()
    v_copies = [z_copy(1, slot, values, v_all.at[slot, x]) for slot in range(1, ring_z)]
    own_v = pltpu.make_async_copy(values.at[:, head_cols(z)], v_all.at[0, x], own_sem.at[2])
    q_copies = [z_copy(2, slot, queries, q_all.at[slot]) for slot in range(1, ring_z)]

    groups = [(0, 1)] + [(lo, min(lo + 2, ring_z)) for lo in range(1, ring_z, 2)]
    last_group = len(groups) - 1
    x_copies = []

    def near(kind, group, way, array, source):
        lo, hi = groups[group]
        view = array.at[pl.ds(lo, hi - lo), source]
        return pltpu.make_async_remote_copy(
            src_ref=view, dst_ref=view,
            send_sem=x_send.at[kind, group, way], recv_sem=x_recv.at[kind, group, way],
            device_id=(right_id, left_id)[way], device_id_type=MESH,
        )

    def further(kind, group, way, array, source):
        lo, hi = groups[group]
        view = array.at[pl.ds(lo, hi - lo), source, pl.ds(way * half, half)]
        return pltpu.make_async_remote_copy(
            src_ref=view, dst_ref=view,
            send_sem=far_send.at[kind, group, way], recv_sem=far_recv.at[kind, group, way],
            device_id=(right_id, left_id)[way], device_id_type=MESH,
        )

    def first_hop(kind, group):
        array, copies, own = ((k_all, k_copies, own_k), (v_all, v_copies, own_v))[kind]
        lo, hi = groups[group]
        if lo == 0:
            own.wait()
        else:
            for slot in range(lo, hi):
                copies[slot - 1].wait_recv()
        for way in range(2):
            copy = near(kind, group, way, array, x)
            copy.start()
            x_copies.append(copy)

    def second_hop(kind, group):
        array = (k_all, v_all)[kind]
        for way in range(2):
            near(kind, group, way, array, (left, right)[way]).wait_recv()
            copy = further(kind, group, way, array, (left, right)[way])
            copy.start()
            x_copies.append(copy)

    def arrived(kind):
        for group in range(len(groups)):
            for way in range(2):
                further(kind, group, way, (k_all, v_all)[kind], far).wait_recv()

    first_hop(0, 0)

    for start in inside[before:]:
        convolve(start)
    waiting = [functools.partial(first_hop, 0, group) for group in range(1, len(groups))]

    def pump(count):
        for _ in range(min(count, len(waiting))):
            waiting.pop(0)()

    pump(1)
    halo.wait_recv()
    wide[:, pl.ds(0, HALO)] = hyena_buf[:, pl.ds(0, HALO)].astype(F32)
    product_only(8)
    convolve(HALO)
    convolve(HALO + 8)
    for start in range(0, rows, 16):
        stream = (in_buf[pl.ds(start, 16), :].astype(F32) + gate_free[pl.ds(start, 16), :]).astype(BF16)
        stream_buf[pl.ds(start, 16), :] = stream
        stream = stream.astype(F32)
        square = stream * stream
        folded = square[:, 0:128]
        for lane in range(128, channels, 128):
            folded = folded + square[:, lane:lane + 128]
        total_col[pl.ds(start, 16), :] = folded
    store_s = pltpu.make_async_copy(stream_buf, stream_out, load_sem.at[0])
    store_s.start()

    padded = total_col.shape[0]
    if padded > rows:
        total_col[pl.ds(rows, padded - rows), :] = jnp.zeros((padded - rows, 128), F32)
    for start in range(0, padded, 128):
        turned = total_col[pl.ds(start, 128), :].T
        row = jnp.sum(turned, axis=0, keepdims=True)
        sums[tp, :, pl.ds(start, 128)] = jnp.broadcast_to(row, (8, 128))
    sum_copies = []
    for step in range(1, ring_tp):
        copy = pltpu.make_async_remote_copy(
            src_ref=sums.at[tp], dst_ref=sums.at[tp],
            send_sem=sum_send.at[step], recv_sem=sum_recv.at[step],
            device_id=(ctx, (tp + step) % ring_tp), device_id_type=MESH,
        )
        copy.start()
        sum_copies.append(copy)
    early = min(EARLY, ring_z - 1)
    for copy in q_copies[:early]:
        copy.start()

    waiting[1:1] = [functools.partial(second_hop, 0, 0)]
    waiting[3:3] = [functools.partial(second_hop, 0, 1)]
    pump(K_PUMPS)

    def query_columns(slot, carry):
        row_z = (z + jnp.where(slot % 2 == 1, (slot + 1) // 2, ring_z - slot // 2)) % ring_z
        begin = columns(row_z * RING_X + x)
        seg_query[slot] = turn_buf[pl.ds(begin, rows), :]
        return carry

    lax.fori_loop(1, ring_z, query_columns, 0)
    total = sums[tp]
    for copy in sum_copies:
        copy.wait_recv()
    for step in range(1, ring_tp):
        total = total + sums[(tp + step) % ring_tp]
    scale = lax.rsqrt(total / (channels * ring_tp) + EPSILON)
    for start in range(0, padded, 128):
        row = jnp.broadcast_to(scale[0:1, start:start + 128], (128, 128))
        total_col[pl.ds(start, 128), :] = row.T
    for start in range(0, rows, 16):
        norm = tile_lanes(total_col[pl.ds(start, 16), :])
        values[pl.ds(start, 16), :] = (stream_buf[pl.ds(start, 16), :].astype(F32) * norm).astype(BF16)

    for copy in v_copies:
        copy.start()
    own_v.start()
    for copy in q_copies[early:]:
        copy.start()
    waiting += [functools.partial(second_hop, 0, group) for group in range(2, len(groups))]
    waiting += [functools.partial(first_hop, 1, 0)]
    pump(len(waiting))

    for group in range(1, len(groups) + 2):
        if group < len(groups):
            waiting.append(functools.partial(first_hop, 1, group))
        if group >= 2:
            waiting.append(functools.partial(second_hop, 1, group - 2))
    pump(1)
    arrived(0)

    def tile_of(array, row_z):
        slot = slot_of((row_z - z + ring_z) % ring_z, ring_z)
        return array[slot].reshape(span, HEAD_DIM)

    def weigh(slot, relays):
        row_z = z_at(offsets[slot])
        low = jnp.maximum(row_z - reach, 0)

        def score(index, carry):
            scores_buf[index - low] = lax.dot_general(
                q_all[slot], tile_of(k_all, index), (((1,), (1,)), ((), ())),
                preferred_element_type=F32,
            )
            return carry

        @pl.when(row_z < reach)
        def _():
            lax.fori_loop(0, row_z + 1, score, 0)

        @pl.when(row_z >= reach)
        def _():
            for index in range(reach + 1):
                score(low + index, 0)

        pump(relays)

        def mask_tile(index, top, diagonal):
            documents = jnp.concatenate(
                [seg_buf[pl.ds(index * lane_rows + i, 1), :] for i in range(lane_rows)], axis=1
            ).astype(F32)
            tops = []
            for start in range(0, rows, CHUNK):
                here = jnp.concatenate([seg_query[slot, pl.ds(start, CHUNK), :]] * lane_rows, axis=1)
                allowed = here == documents
                if diagonal:
                    row_at = x * rows + start + lax.broadcasted_iota(jnp.int32, (CHUNK, span), 0)
                    allowed = allowed & (lax.broadcasted_iota(jnp.int32, (CHUNK, span), 1) <= row_at)
                scores = jnp.where(allowed, scores_buf[index - low, pl.ds(start, CHUNK), :], -BIG)
                scores_buf[index - low, pl.ds(start, CHUNK), :] = scores
                most_here = top[start:start + CHUNK]
                for lane in range(0, span, 128):
                    most_here = jnp.maximum(most_here, scores[:, lane:lane + 128])
                tops.append(most_here)
            return jnp.concatenate(tops, axis=0)

        def largest(top):
            top = mask_tile(row_z, top, True)
            top_buf[...] = jnp.broadcast_to(jnp.max(top, axis=1, keepdims=True), (rows, 128))

        @pl.when(row_z < reach)
        def _():
            largest(lax.fori_loop(
                0, row_z, lambda index, top: mask_tile(index, top, False),
                jnp.full((rows, 128), -BIG, F32),
            ))

        @pl.when(row_z >= reach)
        def _():
            top = jnp.full((rows, 128), -BIG, F32)
            for index in range(reach):
                top = mask_tile(low + index, top, False)
            largest(top)

        def term_tile(index, totals):
            parts = []
            for start in range(0, rows, CHUNK):
                total_here = totals[start:start + CHUNK]
                top = top_buf[pl.ds(start, CHUNK), :]
                for lane in range(0, span, 128):
                    scores = scores_buf[index, pl.ds(start, CHUNK), lane:lane + 128]
                    terms = jnp.exp2((scores - top) * factor)
                    total_here = total_here + terms
                    terms_buf[slot, index, pl.ds(start, CHUNK), lane:lane + 128] = terms.astype(BF16)
                parts.append(total_here)
            return jnp.concatenate(parts, axis=0)

        def divide_by(totals):
            inverse[slot] = jnp.broadcast_to(1.0 / jnp.sum(totals, axis=1, keepdims=True), (rows, 128))

        @pl.when(row_z < reach)
        def _():
            divide_by(lax.fori_loop(0, row_z + 1, term_tile, jnp.zeros((rows, 128), F32)))

        @pl.when(row_z >= reach)
        def _():
            totals = jnp.zeros((rows, 128), F32)
            for index in range(reach + 1):
                totals = term_tile(index, totals)
            divide_by(totals)

    def add_up(slot):
        row_z = z_at(offsets[slot])
        low = jnp.maximum(row_z - reach, 0)

        def add_tile(index, carry):
            summed[...] += jnp.dot(
                terms_buf[slot, index - low], tile_of(v_all, index), preferred_element_type=F32
            )
            return carry

        @pl.when(row_z < reach)
        def _():
            summed[...] = jnp.zeros((rows, HEAD_DIM), F32)
            lax.fori_loop(0, row_z + 1, add_tile, 0)

        @pl.when(row_z >= reach)
        def _():
            total = None
            for index in range(reach + 1):
                part = jnp.dot(
                    terms_buf[slot, index], tile_of(v_all, low + index), preferred_element_type=F32
                )
                total = part if total is None else total + part
            summed[...] = total

        results[slot] = (summed[...] * inverse[slot]).astype(BF16)

    back_copies = []

    def give_back(slot):
        copy = pltpu.make_async_remote_copy(
            src_ref=results.at[slot], dst_ref=attended.at[:, head_cols(z)],
            send_sem=back_send.at[slot], recv_sem=back_recv.at[slot],
            device_id=(z_at(offsets[slot]) * RING_X + x, tp), device_id_type=MESH,
        )
        copy.start()
        back_copies.append(copy)

    own_q.wait()
    for slot in range(ring_z):
        if slot > 0:
            q_copies[slot - 1].wait_recv()
        inside_it, after_it = V_PUMPS[slot] if slot < len(V_PUMPS) else (0, 0)
        weigh(slot, inside_it)
        pump(after_it)
    pump(len(waiting))
    arrived(1)
    for slot in reversed(range(ring_z)):
        add_up(slot)
        if slot > 0:
            give_back(slot)
    own_o = pltpu.make_async_copy(results.at[0], attended.at[:, head_cols(z)], own_sem.at[0])
    own_o.start()
    own_o.wait()
    for slot in range(1, ring_z):
        pltpu.make_async_remote_copy(
            src_ref=results.at[slot], dst_ref=attended.at[:, head_cols(z_at(-offsets[slot]))],
            send_sem=back_send.at[slot], recv_sem=back_recv.at[slot],
            device_id=(z_at(offsets[slot]) * RING_X + x, tp), device_id_type=MESH,
        ).wait_recv()
    store_s.wait()
    halo.wait_send()
    for copy in sum_copies + k_copies + v_copies + q_copies + x_copies + back_copies:
        copy.wait_send()


def place_kernel(stream_from, attended_from, stream, attended, sem):
    copies = [
        pltpu.make_async_copy(stream_from, stream, sem.at[0]),
        pltpu.make_async_copy(attended_from, attended, sem.at[1]),
    ]
    for copy in copies:
        copy.start()
    for copy in copies:
        copy.wait()


ANY = pl.BlockSpec(memory_space=pl.ANY)
HBM = pl.BlockSpec(memory_space=pltpu.HBM)


def body(ring_ctx, ring_tp, most, hyena_in, stream_in, feat_filter, inner_filter, queries, key_vectors, segments):
    rows, channels = stream_in.shape
    ring_z = ring_ctx // RING_X
    tokens = segments.shape[0]
    hyena = jnp.transpose(hyena_in, (1, 0, 2))
    padded = -(-rows // 128) * 128
    span = RING_X * rows
    tiles = -(-most // span) + 1
    groups = 1 + ring_z // 2
    turned = 128 * (-(-rows // 128) + 1)
    dma = pltpu.SemaphoreType.DMA
    block = pltpu.VMEM((rows, channels), BF16)
    gathered = pltpu.VMEM((ring_z, RING_X, rows, HEAD_DIM), BF16)
    by_row = (ring_z, rows, HEAD_DIM)
    out = jax.ShapeDtypeStruct((rows, channels), BF16)
    results = pl.pallas_call(
        functools.partial(mixer_kernel, ring_z, ring_tp, rows, most),
        name="mixer",
        out_shape=(out, out),
        in_specs=[HBM] * 7,
        out_specs=(ANY, ANY),
        scratch_shapes=[
            pltpu.VMEM((3, HALO + rows, channels), BF16),
            pltpu.VMEM((3, HALO + rows, channels), F32),
            pltpu.VMEM((HALO + rows, channels), F32),
            pltpu.VMEM((rows, channels), F32),
            block, block, block,
            pltpu.VMEM(feat_filter.shape, F32),
            pltpu.VMEM(inner_filter.shape, F32),
            pltpu.VMEM((tokens // 128, 128), jnp.int32),
            pltpu.VMEM((turned, 128), F32),
            pltpu.VMEM((HALO + rows, 128), F32),
            pltpu.VMEM((ring_z, rows, 128), F32),
            pltpu.VMEM((ring_tp, 8, padded), F32),
            pltpu.VMEM((padded, 128), F32),
            pltpu.VMEM(by_row, BF16),
            gathered, gathered,
            pltpu.VMEM((tiles, rows, span), F32),
            pltpu.VMEM((ring_z, tiles, rows, span), BF16),
            pltpu.VMEM(by_row, F32),
            pltpu.VMEM((rows, 128), F32),
            pltpu.VMEM((rows, HEAD_DIM), F32),
            pltpu.VMEM(by_row, BF16),
            dma((5,)), dma((3,)), dma((2,)), dma((ring_tp,)), dma((ring_tp,)),
            dma((3, ring_z)), dma((3, ring_z)),
            dma((2, groups, 2)), dma((2, groups, 2)),
            dma((2, groups, 2)), dma((2, groups, 2)),
            dma((ring_z,)), dma((ring_z,)),
        ],
        compiler_params=pltpu.CompilerParams(
            collective_id=0, has_side_effects=True, vmem_limit_bytes=48 * 1024 * 1024
        ),
    )(*(
        pltpu.with_memory_space_constraint(value, pltpu.HBM)
        for value in (
            hyena, stream_in, feat_filter, inner_filter, queries, key_vectors,
            segments.reshape(tokens // 128, 128),
        )
    ))
    return pl.pallas_call(
        place_kernel,
        name="place",
        out_shape=(out, out),
        in_specs=[ANY] * 2,
        out_specs=(ANY, ANY),
        scratch_shapes=[dma((2,))],
        compiler_params=pltpu.CompilerParams(vmem_limit_bytes=48 * 1024 * 1024),
    )(*results)


def solution(mesh):
    in_specs = (
        P("ctx", None, "tp"),
        P("ctx", "tp"),
        P(None, None, "tp"),
        P(None, "tp"),
        P("ctx", "tp"),
        P("ctx", "tp"),
        P(),
    )
    out_specs = (P("ctx", "tp"), P("ctx", "tp"))

    def whole(*args):
        most = args[-1].shape[0] // 2
        mapped = jax.shard_map(
            functools.partial(body, mesh.shape["ctx"], mesh.shape["tp"], most),
            mesh=mesh, in_specs=in_specs, out_specs=out_specs, check_vma=False,
        )
        return mapped(*args)

    return whole
```
